256 devices in a mesh: dom: 8 (over x, core), fsdp: 32 (over y, z).
Axes of the slice: x: 4, y: 4, z: 8, core: 2. Of those that a mesh axis runs over, the one named last changes fastest.
Arguments:
- node_state: bfloat16 [196608, 256], P(('dom', 'fsdp')), may hold values from -6 to 6
- edge_state: bfloat16 [524288, 256], P(('dom', 'fsdp')), may hold values from -6 to 6
- cotangent: bfloat16 [196608, 256], P(('dom', 'fsdp')), may hold values from -6 to 6
- w_first: bfloat16 [768, 256], P('fsdp'), may hold values from -0.21875 to 0.21875
- w_second: bfloat16 [256, 256], P('fsdp'), may hold values from -0.375 to 0.375
- w_third: bfloat16 [256, 256], P('fsdp'), may hold values from -0.375 to 0.375
- pair_near: int32 [4096], P(('dom', 'fsdp')), may hold values from 0 to 5
- pair_far: int32 [4096], P(('dom', 'fsdp')), may hold values from 0 to 9, as said below
- send_fsdp: int32 [256, 2, 1], P(('dom', 'fsdp')), may hold values from 0 to 5
- send_dom: int32 [256, 2, 1], P(('dom', 'fsdp')), may hold values from 0 to 5
Outputs:
- new_state: bfloat16 [196608, 256], P(('dom', 'fsdp'))
- grad_state: bfloat16 [196608, 256], P(('dom', 'fsdp'))
- grad_edges: bfloat16 [524288, 256], P(('dom', 'fsdp'))
- grad_first: float32 [768, 256], P('fsdp')
- grad_second: float32 [256, 256], P('fsdp')
- grad_third: float32 [256, 256], P('fsdp')
The draws below stay inside these ranges and needn't reach their ends.
Inputs may be any that keep to these rules, and one draw needn't show every extreme that they name: `pair_near`: an own block of the holding device. `pair_far`: an entry of the holding device's extended table; each entry from 6 on is named by exactly one pair of the holding device, the other pairs name own blocks. `send_fsdp`: an own block of the lending device. `send_dom`: an own block of the lending device.
All inputs are finite; a program needn't handle non-finite values.
Results may differ from the reference program's by a relative error of at most 0.024.
Values may be sent and summed in bfloat16 or wider, within the bound.
A program may use at most 64 MiB of HBM per device.

```python
import jax
import jax.numpy as jnp
from jax import lax

D = 256
BLOCK = 128
NBD = 6
EPD = 16
HF = 1
HD = 1
NEXT = 10
NODES = 196608
EDGES = 524288
N_DOM = 8
N_FSDP = 32
DEVICES = 256


def draw_pair_far(key, part):
    key = jax.random.fold_in(key, 11)
    halo_count = 2 * HF + 2 * HD
    device_count = N_DOM * N_FSDP
    local_key, order_key = jax.random.split(key)
    local_part = jax.random.randint(local_key, (device_count, EPD - halo_count), 0, NBD)
    halo_part = jnp.broadcast_to(NBD + jnp.arange(halo_count, dtype=jnp.int32), (device_count, halo_count))
    joined = jnp.concatenate([halo_part, local_part.astype(jnp.int32)], 1)
    order_keys = jax.random.split(order_key, device_count)
    shuffled = jax.vmap(lambda one_key, row: jax.random.permutation(one_key, row))(order_keys, joined)
    return shuffled.reshape(-1).astype(jnp.int32)


def place_ends(entries, stream_key, low, top_value):
    shape = entries.shape
    spot = [jax.random.randint(jax.random.fold_in(stream_key, axis), (), 0, shape[axis]) for axis in range(len(shape))]
    entries = entries.at[tuple(spot)].set(low)
    longest = shape.index(max(shape))
    spot[longest] = (spot[longest] + 1) % shape[longest]
    return entries.at[tuple(spot)].set(top_value)


def shard_levels(key, dims, pieces, least, high):
    factor_of, own = 1.0, jax.random.fold_in(key, 6)
    for position, blocks in pieces:
        heights = jnp.exp(jax.random.uniform(jax.random.fold_in(own, position), (blocks,), jnp.float32, least / len(pieces), high / len(pieces)))
        factor_of = factor_of * jnp.repeat(heights, dims[position] // blocks).reshape([-1 if axis == position else 1 for axis in range(len(dims))])
    return factor_of


def scatter_about(stream_key, dims, width, bound, cuts=(), kind=jnp.bfloat16):
    drawn = width * jax.random.normal(stream_key, dims, jnp.float32)
    if cuts:
        drawn = drawn * shard_levels(stream_key, dims, cuts, -0.22, 0.18)
    return jnp.clip(drawn, -bound, bound).astype(kind)


def setup_inputs(seed: int = 0) -> dict:
    seeds = jax.random.split(jax.random.key(seed), 11)
    return {
        "node_state": scatter_about(seeds[0], (NODES, D), 1.0, 6.0, ((0, 256),)),
        "edge_state": scatter_about(seeds[1], (EDGES, D), 1.0, 6.0, ((0, 256),)),
        "cotangent": scatter_about(seeds[2], (NODES, D), 1.0, 6.0, ((0, 256),)),
        "w_first": scatter_about(seeds[3], (3 * D, D), (3 * D) ** -0.5, 0.21875, ((0, 32),)),
        "w_second": scatter_about(seeds[4], (D, D), D ** -0.5, 0.375, ((0, 32),)),
        "w_third": scatter_about(seeds[5], (D, D), D ** -0.5, 0.375, ((0, 32),)),
        "pair_near": place_ends(jax.random.randint(seeds[6], (DEVICES * EPD,), 0, NBD), jax.random.fold_in(seeds[6], 1), 0, NBD - 1).astype(jnp.int32),
        "pair_far": draw_pair_far(jax.random.fold_in(seeds[10], 71), 0),
        "send_fsdp": place_ends(jax.random.randint(seeds[8], (DEVICES, 2, HF), 0, NBD), jax.random.fold_in(seeds[8], 1), 0, NBD - 1).astype(jnp.int32),
        "send_dom": place_ends(jax.random.randint(seeds[9], (DEVICES, 2, HD), 0, NBD), jax.random.fold_in(seeds[9], 1), 0, NBD - 1).astype(jnp.int32),
    }


def silu_slope(values):
    sigmoid = jax.nn.sigmoid(values)
    return sigmoid * (1.0 + values * (1.0 - sigmoid))


def forward_pass(near_rows, far_rows, edge_rows, w_first, w_second, w_third):
    edge_count = near_rows.shape[0]
    stacked = jnp.concatenate([jnp.concatenate([near_rows, far_rows, edge_rows], 1), jnp.concatenate([far_rows, near_rows, edge_rows], 1)], 0)
    first_pre = jnp.dot(stacked, w_first, preferred_element_type=jnp.float32)
    first_act = jax.nn.silu(first_pre).astype(jnp.bfloat16)
    second_pre = jnp.dot(first_act, w_second, preferred_element_type=jnp.float32)
    second_act = jax.nn.silu(second_pre).astype(jnp.bfloat16)
    message = jnp.dot(second_act, w_third, preferred_element_type=jnp.float32)
    face_flux = message[:edge_count] - message[edge_count:]
    return face_flux, (stacked, first_pre, first_act, second_pre, second_act)


def backward_pass(flux_grad, saved, w_first, w_second, w_third):
    stacked, first_pre, first_act, second_pre, second_act = saved
    edge_count = flux_grad.shape[0]
    latent = w_second.shape[0]
    signed = flux_grad.astype(jnp.bfloat16)
    both_grad = jnp.concatenate([signed, -signed], 0)
    second_grad = (jnp.dot(both_grad, w_third.T, preferred_element_type=jnp.float32) * silu_slope(second_pre)).astype(jnp.bfloat16)
    first_grad = (jnp.dot(second_grad, w_second.T, preferred_element_type=jnp.float32) * silu_slope(first_pre)).astype(jnp.bfloat16)
    forward_part = first_grad[:edge_count]
    mirror_part = first_grad[edge_count:]

    def through(row_block, offset):
        return jnp.dot(row_block, w_first[offset:offset + latent].T, preferred_element_type=jnp.float32)

    near_grad = through(forward_part, 0) + through(mirror_part, latent)
    far_grad = through(forward_part, latent) + through(mirror_part, 0)
    edge_grad = (through(forward_part, 2 * latent) + through(mirror_part, 2 * latent)).astype(jnp.bfloat16)
    grad_third = jnp.dot(second_act.T, both_grad, preferred_element_type=jnp.float32)
    grad_second = jnp.dot(first_act.T, second_grad, preferred_element_type=jnp.float32)
    grad_first = jnp.dot(stacked.T, first_grad, preferred_element_type=jnp.float32)
    return near_grad, far_grad, edge_grad, (grad_first, grad_second, grad_third)


def add_terms(total, near_terms, far_terms, near_local, far_table, local_ids, table_ids):
    near_blocks = jax.ops.segment_sum(near_terms.reshape(EPD, -1), near_local, NBD)
    far_blocks = jax.ops.segment_sum(far_terms.reshape(EPD, -1), far_table, NEXT)
    rounded = lax.optimization_barrier(far_blocks[NBD:].astype(jnp.bfloat16)).astype(jnp.float32)
    far_blocks = jnp.concatenate([far_blocks[:NBD], rounded], 0)
    total = total.at[local_ids].add(near_blocks)
    return total.at[table_ids].add(far_blocks)


def reference(node_state, edge_state, cotangent, w_first, w_second, w_third, pair_near, pair_far, send_fsdp, send_dom):
    node_blocks = node_state.reshape(-1, BLOCK, D)
    cot_blocks = cotangent.reshape(-1, BLOCK, D)
    total_blocks = node_blocks.shape[0]

    def device_step(carry, device):
        state_sum, grad_sum, acc_first, acc_second, acc_third = carry
        dom_index = device // N_FSDP
        fsdp_index = device % N_FSDP
        local_ids = device * NBD + jnp.arange(NBD, dtype=jnp.int32)
        lower_fsdp = (dom_index * N_FSDP + (fsdp_index - 1) % N_FSDP).astype(jnp.int32)
        upper_fsdp = (dom_index * N_FSDP + (fsdp_index + 1) % N_FSDP).astype(jnp.int32)
        lower_dom = (((dom_index - 1) % N_DOM) * N_FSDP + fsdp_index).astype(jnp.int32)
        upper_dom = (((dom_index + 1) % N_DOM) * N_FSDP + fsdp_index).astype(jnp.int32)
        table_ids = jnp.concatenate([
            local_ids,
            lower_fsdp * NBD + send_fsdp[lower_fsdp, 1, :],
            upper_fsdp * NBD + send_fsdp[upper_fsdp, 0, :],
            lower_dom * NBD + send_dom[lower_dom, 1, :],
            upper_dom * NBD + send_dom[upper_dom, 0, :]]).astype(jnp.int32)
        near_local = lax.dynamic_slice_in_dim(pair_near, (device * EPD).astype(jnp.int32), EPD)
        far_table = lax.dynamic_slice_in_dim(pair_far, (device * EPD).astype(jnp.int32), EPD)
        near_ids = local_ids[near_local]
        far_ids = table_ids[far_table]
        near_rows = node_blocks[near_ids].reshape(-1, D)
        far_rows = node_blocks[far_ids].reshape(-1, D)
        edge_rows = lax.dynamic_slice_in_dim(edge_state, (device * EPD * BLOCK).astype(jnp.int32), EPD * BLOCK)
        face_flux, saved = forward_pass(near_rows, far_rows, edge_rows, w_first, w_second, w_third)
        flux_grad = (cot_blocks[near_ids].astype(jnp.float32) - cot_blocks[far_ids].astype(jnp.float32)).reshape(-1, D)
        near_grad, far_grad, edge_grad, grads = backward_pass(flux_grad, saved, w_first, w_second, w_third)
        state_sum = add_terms(state_sum, face_flux, -face_flux, near_local, far_table, local_ids, table_ids)
        grad_sum = add_terms(grad_sum, near_grad, far_grad, near_local, far_table, local_ids, table_ids)
        carry = (state_sum, grad_sum, acc_first + grads[0], acc_second + grads[1], acc_third + grads[2])
        return carry, edge_grad

    start = (jnp.zeros((total_blocks, BLOCK * D), jnp.float32), jnp.zeros((total_blocks, BLOCK * D), jnp.float32),
             jnp.zeros((3 * D, D), jnp.float32), jnp.zeros((D, D), jnp.float32), jnp.zeros((D, D), jnp.float32))
    final, edge_grads = lax.scan(device_step, start, jnp.arange(N_DOM * N_FSDP, dtype=jnp.int32))
    state_sum, grad_sum, grad_first, grad_second, grad_third = final
    new_state = (node_state.astype(jnp.float32) + state_sum.reshape(-1, D)).astype(jnp.bfloat16)
    grad_state = (cotangent.astype(jnp.float32) + grad_sum.reshape(-1, D)).astype(jnp.bfloat16)
    grad_edges = edge_grads.reshape(-1, D)
    return new_state, grad_state, grad_edges, grad_first, grad_second, grad_third
```

```python
import jax
import jax.numpy as jnp
from jax import lax
from jax.experimental import pallas as pl
from jax.experimental.pallas import tpu as pltpu
from jax.sharding import PartitionSpec as P

BLOCK = 128
D = 256
NBD = 6
NH = 4
NEXT = NBD + NH
PAIRS = 16
NX, NY, NZ = 4, 4, 8
NZH = NZ // 2
UNITS = 5
CHUNK = 4
MESH = pl.DeviceIdType.MESH
F32, BF16 = jnp.float32, jnp.bfloat16


def place():
    a = lax.axis_index("dom")
    f = lax.axis_index("fsdp")
    return a, f, a // 2, lax.rem(a, 2), f // NZ, lax.rem(f, NZ)


def halo_peers(a, f):
    nd, nf = 2 * NX, NY * NZ
    return (
        (a, lax.rem(f + nf - 1, nf)),
        (a, lax.rem(f + 1, nf)),
        (lax.rem(a + nd - 1, nd), f),
        (lax.rem(a + 1, nd), f),
    )


def greet(peers):
    barrier = pltpu.get_barrier_semaphore()
    for peer in peers:
        pl.semaphore_signal(barrier, inc=1, device_id=peer, device_id_type=MESH)
    pl.semaphore_wait(barrier, len(peers))


def remote(src, dst, send, recv, peer):
    return pltpu.make_async_remote_copy(
        src_ref=src, dst_ref=dst, send_sem=send, recv_sem=recv,
        device_id=peer, device_id_type=MESH,
    )


def gather_kernel(
    sf, sd, w1, w2, w3, node, cot, wall, halo, lend,
    zs, zr, ys, yr, ss, sr, hs, hr,
):
    a, f, x, c, y, z = place()
    zh, zc = z // 2, lax.rem(z, 2)
    sib = (a + 1 - 2 * c, f)
    zpeers = [(a, y * NZ + lax.rem(z + d, NZ)) for d in range(1, NZ)]
    ypeers = [(a, lax.rem(y + d, NY) * NZ + z) for d in range(1, NY)]
    hpeers = halo_peers(a, f)

    for s in range(2):
        b = sf[s]
        lend[s, 0] = node[b]
        lend[s, 1] = cot[b]
        b = sd[s]
        lend[2 + s, 0] = node[b]
        lend[2 + s, 1] = cot[b]

    @pl.when(zc == c)
    def _():
        wall[y, zh, c, 0:3] = w1[...].astype(F32).reshape(3, 8, D).astype(BF16)
        wall[y, zh, c, 3] = w2[...]
        wall[y, zh, c, 4] = w3[...]

    greet(zpeers + ypeers + [sib] + list(hpeers))

    halos = [
        remote(lend.at[s], halo.at[s ^ 1], hs.at[s], hr.at[s ^ 1], hpeers[s])
        for s in range(NH)
    ]
    zcopies = [
        remote(wall.at[y, zh, c], wall.at[y, zh, c], zs.at[d], zr.at[zh], peer)
        for d, peer in enumerate(zpeers)
    ]

    @pl.when(zc == c)
    def _():
        for copy in zcopies:
            copy.start()

    halos[2].start()
    halos[3].start()

    for h in range(NZH):
        @pl.when(2 * h + c != z)
        def _():
            remote(
                wall.at[y, h, c], wall.at[y, h, c], zs.at[0], zr.at[h], sib
            ).wait_recv()

    def part(yy, cc):
        return wall.at[yy, :, cc]

    ycopies = [
        remote(part(y, c), part(y, c), ys.at[d], yr.at[y], peer)
        for d, peer in enumerate(ypeers)
    ]
    for copy in ycopies:
        copy.start()
    scopies = [remote(part(y, c), part(y, c), ss.at[0], sr.at[0], sib)]
    scopies[0].start()
    halos[0].start()
    halos[1].start()
    for d in range(1, NY):
        yy = lax.rem(y + d, NY)
        remote(part(yy, c), part(yy, c), ys.at[0], yr.at[yy], sib).wait_recv()
        copy = remote(part(yy, c), part(yy, c), ss.at[d], sr.at[d], sib)
        copy.start()
        scopies.append(copy)
    for d in range(NY):
        yy = lax.rem(y + d, NY)
        remote(part(yy, 1 - c), part(yy, 1 - c), ss.at[d], sr.at[d], sib).wait_recv()
    for s in range(NH):
        halos[s].wait_recv()

    @pl.when(zc == c)
    def _():
        for copy in zcopies:
            copy.wait_send()

    for copy in ycopies + scopies + halos:
        copy.wait_send()


def gather(sf, sd, w1, w2, w3, node, cot):
    smem = pl.BlockSpec(memory_space=pltpu.SMEM)
    vmem = pl.BlockSpec(memory_space=pltpu.VMEM)
    dma = pltpu.SemaphoreType.DMA
    return pl.pallas_call(
        gather_kernel,
        out_shape=(
            jax.ShapeDtypeStruct((NY, NZH, 2, UNITS, 8, D), BF16),
            jax.ShapeDtypeStruct((NH, 2, BLOCK, D), BF16),
        ),
        in_specs=[smem, smem] + [vmem] * 5,
        out_specs=(vmem, vmem),
        scratch_shapes=[
            pltpu.VMEM((NH, 2, BLOCK, D), BF16),
            dma((NZ - 1,)), dma((NZH,)), dma((NY - 1,)), dma((NY,)),
            dma((NY,)), dma((NY,)), dma((NH,)), dma((NH,)),
        ],
        compiler_params=pltpu.CompilerParams(
            collective_id=0, has_side_effects=True, vmem_limit_bytes=24 << 20
        ),
        name="gather",
    )(sf, sd, w1, w2, w3, node, cot)


def mm(p, q):
    return jnp.dot(p, q, preferred_element_type=F32)


def mm_t(p, q):
    return lax.dot_general(p, q, (((1,), (1,)), ((), ())), preferred_element_type=F32)


def t_mm(p, q):
    return lax.dot_general(p, q, (((0,), (0,)), ((), ())), preferred_element_type=F32)


def act_slope(half):
    up = 1.0 + jnp.tanh(half)
    act = half * up
    return act, up + act * (2.0 - up)


def compute_kernel(
    near, far, wall, halo, node, cot, edge,
    out_edge, state_part, grad_part, back, grads,
    w1, w1h, w2h, w3, w3h, left, right, ctab, tsum, ysum, a1, d1, gg, sg, dd, ef,
    acc_1, acc_2, acc_3,
):
    step = pl.program_id(0)

    @pl.when(step == 0)
    def _():
        packed = wall[...].astype(F32)
        first = packed[:, 0:3].reshape(3 * D, D)
        w1[...] = first.astype(BF16)
        w1h[...] = (0.5 * first).astype(BF16)
        w2h[...] = (0.5 * packed[:, 3].reshape(D, D)).astype(BF16)
        third = packed[:, 4].reshape(D, D)
        w3[...] = third.astype(BF16)
        w3h[...] = (0.5 * third).astype(BF16)
        own = node[...].reshape(NBD * BLOCK, D)
        lent = halo[:, 0].reshape(NH * BLOCK, D)
        for table, cols in ((left, 0), (right, D)):
            weight = w1h[cols:cols + D]
            table[0:NBD] = mm(own, weight).reshape(NBD, BLOCK, D)
            table[NBD:] = mm(lent, weight).reshape(NH, BLOCK, D)
        ctab[0:NBD] = cot[...]
        ctab[NBD:] = halo[:, 1]
        tsum[...] = jnp.zeros_like(tsum)
        ysum[...] = jnp.zeros_like(ysum)
        acc_1[...] = jnp.zeros_like(acc_1)
        acc_2[...] = jnp.zeros_like(acc_2)
        acc_3[...] = jnp.zeros_like(acc_3)

    pairs = [(near[step * CHUNK + j], far[step * CHUNK + j]) for j in range(CHUNK)]
    rows = [slice(j * BLOCK, (j + 1) * BLOCK) for j in range(CHUNK)]
    half = CHUNK * BLOCK
    mirror = [slice(half + j * BLOCK, half + (j + 1) * BLOCK) for j in range(CHUNK)]

    edge_part = mm(edge[...], w1h[2 * D:])
    for j, (n, t) in enumerate(pairs):
        gg[rows[j]] = (ctab[n].astype(F32) - ctab[t].astype(F32)).astype(BF16)
        for where, p, q in ((rows[j], n, t), (mirror[j], t, n)):
            act, slope = act_slope(left[p] + right[q] + edge_part[rows[j]])
            a1[where] = act.astype(BF16)
            d1[where] = slope
    second = mm(a1[...], w2h[...])
    back_3 = mm_t(gg[...], w3h[...])
    for j, (n, t) in enumerate(pairs):
        act_f, slope_f = act_slope(second[rows[j]])
        act_m, slope_m = act_slope(second[mirror[j]])
        diff = act_f.astype(BF16).astype(F32) - act_m.astype(BF16).astype(F32)
        dd[rows[j]] = diff.astype(BF16)
        tsum[n] = tsum[n] + diff
        tsum[t] = tsum[t] - diff
        sg[rows[j]] = (back_3[rows[j]] * slope_f).astype(BF16)
        sg[mirror[j]] = (-back_3[rows[j]] * slope_m).astype(BF16)
    first_back = mm_t(sg[...], w2h[...])
    for j, (n, t) in enumerate(pairs):
        part_f = (first_back[rows[j]] * d1[rows[j]]).astype(BF16).astype(F32)
        part_m = (first_back[mirror[j]] * d1[mirror[j]]).astype(BF16).astype(F32)
        ef[rows[j]] = (part_f + part_m).astype(BF16)
        ysum[0, n] = ysum[0, n] + part_f
        ysum[0, t] = ysum[0, t] + part_m
        ysum[1, n] = ysum[1, n] + part_m
        ysum[1, t] = ysum[1, t] + part_f
    out_edge[...] = mm_t(ef[...], w1[2 * D:]).astype(BF16)
    acc_3[...] += t_mm(dd[...], gg[...])
    acc_2[...] += t_mm(a1[...], sg[...])
    acc_1[2 * D:] += t_mm(edge[...], ef[...])

    @pl.when(step == PAIRS // CHUNK - 1)
    def _():
        own_rows = NBD * BLOCK
        flux = mm(tsum[...].astype(BF16).reshape(NEXT * BLOCK, D), w3[...])
        state_part[...] = node[...].astype(F32) + flux[:own_rows].reshape(NBD, BLOCK, D)
        back[:, 0] = flux[own_rows:].astype(BF16).reshape(NH, BLOCK, D)
        ya = ysum[0].astype(BF16).reshape(NEXT * BLOCK, D)
        yb = ysum[1].astype(BF16).reshape(NEXT * BLOCK, D)
        node_grad = mm_t(ya, w1[0:D]) + mm_t(yb, w1[D:2 * D])
        grad_part[...] = cot[...].astype(F32) + node_grad[:own_rows].reshape(NBD, BLOCK, D)
        back[:, 1] = node_grad[own_rows:].astype(BF16).reshape(NH, BLOCK, D)
        own = node[...].reshape(own_rows, D)
        lent = halo[:, 0].reshape(NH * BLOCK, D)
        acc_1[0:D] = t_mm(own, ya[:own_rows]) + t_mm(lent, ya[own_rows:])
        acc_1[D:2 * D] = t_mm(own, yb[:own_rows]) + t_mm(lent, yb[own_rows:])
        grads[:, 0:3] = acc_1[...].reshape(NY * NZ, 3, 8, D).astype(BF16)
        grads[:, 3] = acc_2[...].reshape(NY * NZ, 8, D).astype(BF16)
        grads[:, 4] = acc_3[...].reshape(NY * NZ, 8, D).astype(BF16)


def compute(near, far, wall, halo, node, cot, edge):
    smem = pl.BlockSpec(memory_space=pltpu.SMEM)
    vmem = pl.BlockSpec(memory_space=pltpu.VMEM)
    chunk = pl.BlockSpec((CHUNK * BLOCK, D), lambda i: (i, 0))
    rows = CHUNK * BLOCK
    table = pltpu.VMEM((NEXT, BLOCK, D), F32)
    return pl.pallas_call(
        compute_kernel,
        grid=(PAIRS // CHUNK,),
        out_shape=(
            jax.ShapeDtypeStruct(edge.shape, BF16),
            jax.ShapeDtypeStruct((NBD, BLOCK, D), F32),
            jax.ShapeDtypeStruct((NBD, BLOCK, D), F32),
            jax.ShapeDtypeStruct((NH, 2, BLOCK, D), BF16),
            jax.ShapeDtypeStruct((NY * NZ, UNITS, 8, D), BF16),
        ),
        in_specs=[smem, smem] + [vmem] * 4 + [chunk],
        out_specs=(chunk, vmem, vmem, vmem, vmem),
        scratch_shapes=[
            pltpu.VMEM((3 * D, D), BF16), pltpu.VMEM((3 * D, D), BF16),
            pltpu.VMEM((D, D), BF16), pltpu.VMEM((D, D), BF16), pltpu.VMEM((D, D), BF16),
            table, table, pltpu.VMEM((NEXT, BLOCK, D), BF16),
            table, pltpu.VMEM((2, NEXT, BLOCK, D), F32),
            pltpu.VMEM((2 * rows, D), BF16), pltpu.VMEM((2 * rows, D), F32),
            pltpu.VMEM((rows, D), BF16), pltpu.VMEM((2 * rows, D), BF16),
            pltpu.VMEM((rows, D), BF16), pltpu.VMEM((rows, D), BF16),
            pltpu.VMEM((3 * D, D), F32), pltpu.VMEM((D, D), F32), pltpu.VMEM((D, D), F32),
        ],
        compiler_params=pltpu.CompilerParams(vmem_limit_bytes=48 << 20),
        name="layer",
    )(near, far, wall, halo, node, cot, edge)


def reduce_kernel(
    sf, sd, grads, state_part, grad_part, back, new_state, grad_state, total,
    got, sibbuf, q, xbuf, r, ybuf, t, zbuf, fin, finbuf,
    hs, hr, ss, sr, xs, xr, ys, yr, zs, zr, fs, fr,
):
    a, f, x, c, y, z = place()
    sib = (a + 1 - 2 * c, f)
    xpeers = [(2 * lax.rem(x + d, NX) + c, f) for d in range(1, NX)]
    ypeers = [(a, lax.rem(y + d, NY) * NZ + z) for d in range(1, NY)]
    zpeers = [(a, y * NZ + lax.rem(z + d, NZ)) for d in range(1, NZ)]
    dpeers = [(lax.rem(a + d, 2 * NX), f) for d in range(1, 2 * NX)]
    hpeers = halo_peers(a, f)
    greet(dpeers + ypeers + zpeers + list(hpeers))

    copy_s = remote(grads.at[:, :, 1 - c], sibbuf, ss, sr, sib)
    copy_s.start()
    halos = [
        remote(back.at[s], got.at[s ^ 1], hs.at[s], hr.at[s ^ 1], hpeers[s])
        for s in range(NH)
    ]
    for copy in halos:
        copy.start()

    copy_s.wait_recv()
    q[...] = (grads[:, :, c].astype(F32) + sibbuf[...].astype(F32)).astype(BF16)
    xcopies = []
    for d, peer in enumerate(xpeers):
        copy = remote(q.at[:, lax.rem(x + d + 1, NX)], xbuf.at[d], xs.at[d], xr.at[d], peer)
        copy.start()
        xcopies.append(copy)

    for copy in halos:
        copy.wait_recv()
    owner = (sf[0], sf[1], sd[0], sd[1])
    for b in range(NBD):
        for k, (part, out) in enumerate(((state_part, new_state), (grad_part, grad_state))):
            value = part[b]
            for s in range(NH):
                value = value + jnp.where(owner[s] == b, got[s, k].astype(F32), 0.0)
            out[b] = value.astype(BF16)

    value = q[:, x].astype(F32)
    for d, copy in enumerate(xcopies):
        copy.wait_recv()
        value = value + xbuf[d].astype(F32)
    r[...] = value.astype(BF16)
    ycopies = []
    for d, peer in enumerate(ypeers):
        copy = remote(r.at[lax.rem(y + d + 1, NY)], ybuf.at[d], ys.at[d], yr.at[d], peer)
        copy.start()
        ycopies.append(copy)
    value = r[y].astype(F32)
    for d, copy in enumerate(ycopies):
        copy.wait_recv()
        value = value + ybuf[d].astype(F32)
    t[...] = value.astype(BF16)

    copy_z = remote(t, zbuf.at[z], zs, zr.at[z], (a, y * NZ + a))
    fcopies = [
        remote(fin, finbuf, fs.at[d], fr, peer) for d, peer in enumerate(dpeers)
    ]

    @pl.when(z != a)
    def _():
        copy_z.start()
        remote(fin, finbuf, fs.at[0], fr, sib).wait_recv()
        total[...] = finbuf[...].astype(F32)

    @pl.when(z == a)
    def _():
        acc = t[...].astype(F32)
        for d in range(1, NZ):
            zz = lax.rem(z + d, NZ)
            remote(t, zbuf.at[zz], zs, zr.at[zz], sib).wait_recv()
            acc = acc + zbuf[zz].astype(F32)
        fin[...] = acc.astype(BF16)
        for copy in fcopies:
            copy.start()
        total[...] = fin[...].astype(F32)

    copy_s.wait_send()
    for copy in halos + xcopies + ycopies:
        copy.wait_send()

    @pl.when(z != a)
    def _():
        copy_z.wait_send()

    @pl.when(z == a)
    def _():
        for copy in fcopies:
            copy.wait_send()


def reduce(sf, sd, grads, state_part, grad_part, back):
    smem = pl.BlockSpec(memory_space=pltpu.SMEM)
    vmem = pl.BlockSpec(memory_space=pltpu.VMEM)
    dma = pltpu.SemaphoreType.DMA
    shard = (UNITS, 8, D)
    return pl.pallas_call(
        reduce_kernel,
        out_shape=(
            jax.ShapeDtypeStruct((NBD, BLOCK, D), BF16),
            jax.ShapeDtypeStruct((NBD, BLOCK, D), BF16),
            jax.ShapeDtypeStruct(shard, F32),
        ),
        in_specs=[smem, smem] + [vmem] * 4,
        out_specs=(vmem, vmem, vmem),
        scratch_shapes=[
            pltpu.VMEM((NH, 2, BLOCK, D), BF16),
            pltpu.VMEM((NY, NZH, *shard), BF16), pltpu.VMEM((NY, NZH, *shard), BF16),
            pltpu.VMEM((NX - 1, NY, *shard), BF16), pltpu.VMEM((NY, *shard), BF16),
            pltpu.VMEM((NY - 1, *shard), BF16), pltpu.VMEM(shard, BF16),
            pltpu.VMEM((NZ, *shard), BF16), pltpu.VMEM(shard, BF16), pltpu.VMEM(shard, BF16),
            dma((NH,)), dma((NH,)), dma, dma,
            dma((NX - 1,)), dma((NX - 1,)), dma((NY - 1,)), dma((NY - 1,)),
            dma, dma((NZ,)), dma((2 * NX - 1,)), dma,
        ],
        compiler_params=pltpu.CompilerParams(
            collective_id=1, has_side_effects=True, vmem_limit_bytes=32 << 20
        ),
        name="reduce",
    )(sf, sd, grads, state_part, grad_part, back)


def body(node_state, edge_state, cotangent, w_first, w_second, w_third,
         pair_near, pair_far, send_fsdp, send_dom):
    node = node_state.reshape(NBD, BLOCK, D)
    cot = cotangent.reshape(NBD, BLOCK, D)
    sf = send_fsdp.reshape(2)
    sd = send_dom.reshape(2)
    wall, halo = gather(sf, sd, w_first, w_second, w_third, node, cot)
    grad_edges, state_part, grad_part, back, grads = compute(
        pair_near, pair_far, wall.reshape(NY * NZ, UNITS, 8, D), halo, node, cot, edge_state
    )
    new_state, grad_state, total = reduce(
        sf, sd, grads.reshape(NY, NZH, 2, UNITS, 8, D), state_part, grad_part, back
    )
    return (
        new_state.reshape(NBD * BLOCK, D),
        grad_state.reshape(NBD * BLOCK, D),
        grad_edges,
        total[0:3].reshape(24, D),
        total[3],
        total[4],
    )


def solution(mesh):
    cells = P(("dom", "fsdp"), None)
    rows = P("fsdp", None)
    flat = P(("dom", "fsdp"))
    lists = P(("dom", "fsdp"), None, None)
    return jax.shard_map(
        body,
        mesh=mesh,
        in_specs=(cells, cells, cells, rows, rows, rows, flat, flat, lists, lists),
        out_specs=(cells, cells, cells, rows, rows, rows),
        check_vma=False,
    )
```

```python
import jax
import jax.numpy as jnp
from jax import lax
from jax.experimental import pallas as pl
from jax.experimental.pallas import tpu as pltpu
from jax.sharding import PartitionSpec as P

BLOCK = 128
D = 256
NBD = 6
NH = 4
NEXT = NBD + NH
PAIRS = 16
NX, NY, NZ = 4, 4, 8
NZH = NZ // 2
UNITS = 5
CHUNK = 4
UNROLL = False
VMEM_MIB = 58
MESH = pl.DeviceIdType.MESH
F32, BF16 = jnp.float32, jnp.bfloat16


def place():
    a = lax.axis_index("dom")
    f = lax.axis_index("fsdp")
    return a, f, a // 2, lax.rem(a, 2), f // NZ, lax.rem(f, NZ)


def halo_peers(a, f):
    nd, nf = 2 * NX, NY * NZ
    return (
        (a, lax.rem(f + nf - 1, nf)),
        (a, lax.rem(f + 1, nf)),
        (lax.rem(a + nd - 1, nd), f),
        (lax.rem(a + 1, nd), f),
    )


def signal_all(peers):
    barrier = pltpu.get_barrier_semaphore()
    for peer in peers:
        pl.semaphore_signal(barrier, inc=1, device_id=peer, device_id_type=MESH)


def wait_all(count):
    pl.semaphore_wait(pltpu.get_barrier_semaphore(), count)


def remote(src, dst, send, recv, peer):
    return pltpu.make_async_remote_copy(
        src_ref=src, dst_ref=dst, send_sem=send, recv_sem=recv,
        device_id=peer, device_id_type=MESH,
    )


def mm(p, q):
    return jnp.dot(p, q, preferred_element_type=F32)


def mm_t(p, q):
    return lax.dot_general(p, q, (((1,), (1,)), ((), ())), preferred_element_type=F32)


def t_mm(p, q):
    return lax.dot_general(p, q, (((0,), (0,)), ((), ())), preferred_element_type=F32)


def act_slope(half):
    up = 1.0 + jnp.tanh(half)
    act = half * up
    return act, up + act * (2.0 - up)


def layer_kernel(
    near_hbm, far_hbm, sf_hbm, sd_hbm, w1_hbm, w2_hbm, w3_hbm, node_hbm, cot_hbm, edge_hbm,
    state_out, grad_out, edge_out, total_out,
    near, far, sf, sd, chain, last, w1s, w2s, w3s, node, cot, edge, lend, wall, halo,
    w1, w1h, w2h, w3, w3h, left, right, ctab, tsum, ysum, a1, d1, gg, sg, dd, ef,
    first, grads, back, state_part, grad_part,
    got, sibbuf, q, xbuf, r, ybuf, t, zbuf, fin, finbuf, new_state, grad_state, ge, total,
    os, ls, zs, zr, ys, yr, ss, sr, hs, hr, bs, br, s0, r0, xs, xr, y2s, y2r, z2s, z2r, fs, fr,
):
    a, f, x, c, y, z = place()
    zh, zc = z // 2, lax.rem(z, 2)
    sib = (a + 1 - 2 * c, f)
    xpeers = [(2 * lax.rem(x + d, NX) + c, f) for d in range(1, NX)]
    ypeers = [(a, lax.rem(y + d, NY) * NZ + z) for d in range(1, NY)]
    zpeers = [(a, y * NZ + lax.rem(z + d, NZ)) for d in range(1, NZ)]
    dpeers = [(lax.rem(a + d, 2 * NX), f) for d in range(1, 2 * NX)]
    hpeers = halo_peers(a, f)
    everyone = zpeers + ypeers + dpeers + list(hpeers)
    signal_all(everyone)

    loads = [
        pltpu.make_async_copy(src, dst, ls.at[i])
        for i, (src, dst) in enumerate((
            (w1_hbm, w1s), (w2_hbm, w2s), (w3_hbm, w3s), (sf_hbm, sf), (sd_hbm, sd),
            (node_hbm, node), (cot_hbm, cot), (near_hbm, near), (far_hbm, far), (edge_hbm, edge),
        ))
    ]
    for copy in loads:
        copy.start()
    for copy in loads[:3]:
        copy.wait()

    @pl.when(zc == c)
    def _():
        wall[y, zh, c, 0:3] = w1s[...].astype(F32).reshape(3, 8, D).astype(BF16)
        wall[y, zh, c, 3] = w2s[...]
        wall[y, zh, c, 4] = w3s[...]

    for copy in loads[3:7]:
        copy.wait()
    for s in range(2):
        b = sf[s]
        lend[s, 0] = node[b]
        lend[s, 1] = cot[b]
        b = sd[s]
        lend[2 + s, 0] = node[b]
        lend[2 + s, 1] = cot[b]
    wait_all(len(everyone))

    halos = [
        remote(lend.at[s], halo.at[s ^ 1], hs.at[s], hr.at[s ^ 1], hpeers[s])
        for s in range(NH)
    ]
    zcopies = [
        remote(wall.at[y, zh, c], wall.at[y, zh, c], zs.at[d], zr.at[zh], zpeers[d])
        for d in (3, 2, 4, 1, 5, 0, 6)
    ]

    @pl.when(zc == c)
    def _():
        for copy in zcopies:
            copy.start()

    halos[2].start()
    halos[3].start()

    loads[7].wait()
    loads[8].wait()
    keys = [(near, far)[h % 2][h // 2] for h in range(2 * PAIRS)]

    def link(h, carry):
        p = h // 2
        key = jnp.where(lax.rem(h, 2) == 0, near[p], far[p])
        before = jnp.int32(2 * PAIRS)
        for g in range(2 * PAIRS):
            before = jnp.where((keys[g] == key) & (g < h), g, before)
        chain[h] = before
        return carry

    lax.fori_loop(0, 2 * PAIRS, link, 0)

    def end(b, carry):
        where = jnp.int32(2 * PAIRS)
        for g in range(2 * PAIRS):
            where = jnp.where(keys[g] == b, g, where)
        last[b] = where
        return carry

    lax.fori_loop(0, NEXT, end, 0)

    sent = []

    def pass_on(yy, h, slot, along_y):
        part = wall.at[yy, h, c]
        if along_y:
            for d, peer in enumerate(ypeers):
                copy = remote(part, part, ys.at[slot, d], yr.at[y, h], peer)
                copy.start()
                sent.append(copy)
        copy = remote(part, part, ss.at[slot], sr.at[yy, h], sib)
        copy.start()
        sent.append(copy)

    for i, d in enumerate((0, 1, 3, 2)):
        h = lax.rem(zh + d, NZH)

        @pl.when(2 * h + c != z)
        def _():
            part = wall.at[y, h, c]
            remote(part, part, zs.at[0], zr.at[h], sib).wait_recv()

        pass_on(y, h, i, True)
    halos[0].start()
    halos[1].start()

    tsum[2 * PAIRS] = jnp.zeros((BLOCK, D), F32)
    ysum[0, 2 * PAIRS] = jnp.zeros((BLOCK, D), F32)
    ysum[1, 2 * PAIRS] = jnp.zeros((BLOCK, D), F32)
    ctab[0:NBD] = cot[...]

    for i, d in enumerate((0, 1, 3, 2)):
        h = lax.rem(zh + d, NZH)
        for e in (1, 3, 2):
            yy = lax.rem(y + e, NY)
            part = wall.at[yy, h, c]
            remote(part, part, ys.at[0, 0], yr.at[yy, h], sib).wait_recv()
            pass_on(yy, h, 4 * e + i, False)
    for s in range(NH):
        halos[s].wait_recv()
    loads[9].wait()
    rows = CHUNK * BLOCK
    direct = [slice(j * BLOCK, (j + 1) * BLOCK) for j in range(CHUNK)]
    mirror = [slice(rows + j * BLOCK, rows + (j + 1) * BLOCK) for j in range(CHUNK)]
    own_rows = NBD * BLOCK
    ctab[NBD:] = halo[:, 1]
    for yy in range(NY):
        for h in range(NZH):
            part = wall.at[yy, h, 1 - c]
            remote(part, part, ss.at[0], sr.at[yy, h], sib).wait_recv()

    packed = wall[...].reshape(NY * NZ, UNITS, 8, D).astype(F32)
    flat = packed[:, 0:3].reshape(3 * D, D)
    w1[...] = flat.astype(BF16)
    w1h[...] = (0.5 * flat).astype(BF16)
    w2h[...] = (0.5 * packed[:, 3].reshape(D, D)).astype(BF16)
    third = packed[:, 4].reshape(D, D)
    w3[...] = third.astype(BF16)
    w3h[...] = (0.5 * third).astype(BF16)
    own = node[...].reshape(own_rows, D)
    lent = halo[:, 0].reshape(NH * BLOCK, D)
    for table, cols in ((left, 0), (right, D)):
        weight = w1h[cols:cols + D]
        table[0:NBD] = mm(own, weight).reshape(NBD, BLOCK, D)
        table[NBD:] = mm(lent, weight).reshape(NH, BLOCK, D)

    def chunk(i, carry):
        pairs = [i * CHUNK + j for j in range(CHUNK)]
        ends = [(near[p], far[p]) for p in pairs]
        links = [(2 * p, chain[2 * p], chain[2 * p + 1]) for p in pairs]
        span = pl.ds(pl.multiple_of(i * rows, rows), rows)
        edge_part = mm(edge[span], w1h[2 * D:])
        for j, (n, m) in enumerate(ends):
            gg[i, direct[j]] = (ctab[n].astype(F32) - ctab[m].astype(F32)).astype(BF16)
            for where, p, k in ((direct[j], n, m), (mirror[j], m, n)):
                act, slope = act_slope(left[p] + right[k] + edge_part[direct[j]])
                a1[i, where] = act.astype(BF16)
                d1[where] = slope
        second = mm(a1[i], w2h[...])
        back_3 = mm_t(gg[i], w3h[...])
        for j, (h, before_n, before_m) in enumerate(links):
            act_f, slope_f = act_slope(second[direct[j]])
            act_m, slope_m = act_slope(second[mirror[j]])
            diff = act_f.astype(BF16).astype(F32) - act_m.astype(BF16).astype(F32)
            dd[i, direct[j]] = diff.astype(BF16)
            tsum[h] = tsum[before_n] + diff
            tsum[h + 1] = tsum[before_m] - diff
            sg[i, direct[j]] = (back_3[direct[j]] * slope_f).astype(BF16)
            sg[i, mirror[j]] = (-back_3[direct[j]] * slope_m).astype(BF16)
        first_back = mm_t(sg[i], w2h[...])
        for j, (h, before_n, before_m) in enumerate(links):
            part_f = (first_back[direct[j]] * d1[direct[j]]).astype(BF16).astype(F32)
            part_m = (first_back[mirror[j]] * d1[mirror[j]]).astype(BF16).astype(F32)
            ef[i, direct[j]] = (part_f + part_m).astype(BF16)
            ysum[0, h] = ysum[0, before_n] + part_f
            ysum[0, h + 1] = ysum[0, before_m] + part_m
            ysum[1, h] = ysum[1, before_n] + part_m
            ysum[1, h + 1] = ysum[1, before_m] + part_f
        ge[span] = mm_t(ef[i], w1[2 * D:]).astype(BF16)
        return carry

    lax.fori_loop(0, PAIRS // CHUNK, chunk, 0, unroll=UNROLL)
    stores = [
        pltpu.make_async_copy(src, dst, os.at[i])
        for i, (src, dst) in enumerate((
            (ge, edge_out), (new_state, state_out), (grad_state, grad_out), (total, total_out),
        ))
    ]
    stores[0].start()

    ends = [last[b] for b in range(NEXT)]

    def gathered(pick):
        return jnp.concatenate([pick(h).astype(BF16) for h in ends], 0)

    ts = gathered(lambda h: tsum[h])
    ya = gathered(lambda h: ysum[0, h])
    yb = gathered(lambda h: ysum[1, h])
    wa, wb = w1[0:D], w1[D:2 * D]

    lent_flux = mm(ts[own_rows:], w3[...])
    lent_grad = mm_t(ya[own_rows:], wa) + mm_t(yb[own_rows:], wb)
    back[:, 0] = lent_flux.astype(BF16).reshape(NH, BLOCK, D)
    back[:, 1] = lent_grad.astype(BF16).reshape(NH, BLOCK, D)
    backs = [
        remote(back.at[s], got.at[s ^ 1], bs.at[s], br.at[s ^ 1], hpeers[s])
        for s in range(NH)
    ]
    for copy in backs:
        copy.start()

    def whole(ref):
        return ref[...].reshape(-1, D)

    pieces = (slice(3, 5), slice(0, 3))

    def to_sibling(k):
        copy = remote(grads.at[:, :, 1 - c, pieces[k]], sibbuf.at[:, :, pieces[k]], s0.at[k], r0.at[k], sib)
        copy.start()
        return copy

    grads[:, :, :, 3] = t_mm(whole(a1), whole(sg)).reshape(NY, NZH, 2, 8, D).astype(BF16)
    grads[:, :, :, 4] = t_mm(whole(dd), whole(gg)).reshape(NY, NZH, 2, 8, D).astype(BF16)
    cores = [to_sibling(0)]
    first[0:D] = t_mm(own, ya[:own_rows]) + t_mm(lent, ya[own_rows:])
    first[D:2 * D] = t_mm(own, yb[:own_rows]) + t_mm(lent, yb[own_rows:])
    first[2 * D:] = t_mm(edge[...], whole(ef))
    grads[:, :, :, 0:3] = first[...].reshape(NY, NZH, 2, 3, 8, D).astype(BF16)
    cores.append(to_sibling(1))

    xcopies = []
    for k, piece in enumerate(pieces):
        if k:
            flux = mm(ts[:own_rows], w3[...]).reshape(NBD, BLOCK, D)
            state_part[...] = node[...].astype(F32) + flux
        cores[k].wait_recv()
        q[:, :, piece] = (grads[:, :, c, piece].astype(F32) + sibbuf[:, :, piece].astype(F32)).astype(BF16)
        for d, peer in enumerate(xpeers):
            xx = lax.rem(x + d + 1, NX)
            copy = remote(q.at[:, xx, piece], xbuf.at[d, :, piece], xs.at[k, d], xr.at[k, d], peer)
            copy.start()
            xcopies.append(copy)

    node_grad = mm_t(ya[:own_rows], wa) + mm_t(yb[:own_rows], wb)
    grad_part[...] = cot[...].astype(F32) + node_grad.reshape(NBD, BLOCK, D)
    value = q[:, x].astype(F32)
    for copy in xcopies:
        copy.wait_recv()
    for d in range(NX - 1):
        value = value + xbuf[d].astype(F32)
    r[...] = value.astype(BF16)
    ycopies = []
    for d, peer in enumerate(ypeers):
        copy = remote(r.at[lax.rem(y + d + 1, NY)], ybuf.at[d], y2s.at[d], y2r.at[d], peer)
        copy.start()
        ycopies.append(copy)

    for copy in backs:
        copy.wait_recv()
    owner = (sf[0], sf[1], sd[0], sd[1])

    def settle(k, part, out):
        for b in range(NBD):
            value = part[b]
            for s in range(NH):
                value = value + jnp.where(owner[s] == b, got[s, k].astype(F32), 0.0)
            out[b] = value.astype(BF16)

    settle(0, state_part, new_state)
    stores[1].start()

    value = r[y].astype(F32)
    for d, copy in enumerate(ycopies):
        copy.wait_recv()
        value = value + ybuf[d].astype(F32)
    t[...] = value.astype(BF16)

    copy_z = remote(t, zbuf.at[z], z2s, z2r.at[z], (a, y * NZ + a))

    @pl.when(z != a)
    def _():
        copy_z.start()

    settle(1, grad_part, grad_state)
    stores[2].start()

    fcopies = [
        remote(fin, finbuf, fs.at[d], fr, peer) for d, peer in enumerate(dpeers)
    ]

    @pl.when(z == a)
    def _():
        acc = t[...].astype(F32)
        for d in range(1, NZ):
            zz = lax.rem(z + d, NZ)
            remote(t, zbuf.at[zz], z2s, z2r.at[zz], sib).wait_recv()
            acc = acc + zbuf[zz].astype(F32)
        fin[...] = acc.astype(BF16)
        for copy in fcopies:
            copy.start()
        total[...] = fin[...].astype(F32)
        for copy in fcopies:
            copy.wait_send()

    @pl.when(z != a)
    def _():
        remote(fin, finbuf, fs.at[0], fr, sib).wait_recv()
        total[...] = finbuf[...].astype(F32)
        copy_z.wait_send()

    @pl.when(zc == c)
    def _():
        for copy in zcopies:
            copy.wait_send()

    stores[3].start()
    for copy in sent + halos + backs + cores + xcopies + ycopies:
        copy.wait_send()
    for copy in stores:
        copy.wait()


def layer(near, far, sf, sd, w1, w2, w3, node, cot, edge):
    hbm = pl.BlockSpec(memory_space=pltpu.HBM)
    dma = pltpu.SemaphoreType.DMA
    steps, rows = PAIRS // CHUNK, CHUNK * BLOCK
    shard = (UNITS, 8, D)

    def smem(count):
        return pltpu.SMEM((count,), jnp.int32)

    def bf(*shape):
        return pltpu.VMEM(shape, BF16)

    def f32(*shape):
        return pltpu.VMEM(shape, F32)

    lent = bf(NH, 2, BLOCK, D)
    blocks = f32(NBD, BLOCK, D)
    return pl.pallas_call(
        layer_kernel,
        out_shape=(
            jax.ShapeDtypeStruct(node.shape, BF16),
            jax.ShapeDtypeStruct(cot.shape, BF16),
            jax.ShapeDtypeStruct(edge.shape, BF16),
            jax.ShapeDtypeStruct(shard, F32),
        ),
        in_specs=[hbm] * 10,
        out_specs=(hbm,) * 4,
        scratch_shapes=[
            smem(PAIRS), smem(PAIRS), smem(2), smem(2), smem(2 * PAIRS), smem(NEXT),
            bf(*w1.shape), bf(*w2.shape), bf(*w3.shape), bf(*node.shape), bf(*cot.shape), bf(*edge.shape),
            lent, bf(NY, NZH, 2, *shard), lent,
            bf(3 * D, D), bf(3 * D, D), bf(D, D), bf(D, D), bf(D, D),
            f32(NEXT, BLOCK, D), f32(NEXT, BLOCK, D), bf(NEXT, BLOCK, D),
            f32(2 * PAIRS + 1, BLOCK, D), f32(2, 2 * PAIRS + 1, BLOCK, D),
            bf(steps, 2 * rows, D), f32(2 * rows, D), bf(steps, rows, D), bf(steps, 2 * rows, D),
            bf(steps, rows, D), bf(steps, rows, D),
            f32(3 * D, D), bf(NY, NZH, 2, *shard), lent, blocks, blocks,
            lent, bf(NY, NZH, *shard), bf(NY, NZH, *shard), bf(NX - 1, NY, *shard), bf(NY, *shard),
            bf(NY - 1, *shard), bf(*shard), bf(NZ, *shard), bf(*shard), bf(*shard),
            bf(*node.shape), bf(*cot.shape), bf(*edge.shape), f32(*shard),
            dma((4,)), dma((10,)), dma((NZ - 1,)), dma((NZH,)), dma((NZH, NY - 1)), dma((NY, NZH)),
            dma((NY * NZH,)), dma((NY, NZH)), dma((NH,)), dma((NH,)), dma((NH,)), dma((NH,)),
            dma((2,)), dma((2,)), dma((2, NX - 1)), dma((2, NX - 1)),
            dma((NY - 1,)), dma((NY - 1,)), dma, dma((NZ,)), dma((2 * NX - 1,)), dma,
        ],
        compiler_params=pltpu.CompilerParams(
            collective_id=0, has_side_effects=True, vmem_limit_bytes=VMEM_MIB << 20
        ),
        name="layer",
    )(near, far, sf, sd, w1, w2, w3, node, cot, edge)


def results_kernel(
    state, grad, edges, total, out_state, out_grad, out_edges, out_1, out_2, out_3,
    state_v, grad_v, edges_v, total_v, in_sem, out_sem,
):
    quarter = edges.shape[0] // 4
    spans = [pl.ds(i * quarter, quarter) for i in range(4)]
    loads, stores = [], []
    for i, (src, held, parts) in enumerate([
        (edges.at[s], edges_v.at[s], [(edges_v.at[s], out_edges.at[s])]) for s in spans
    ] + [
        (state, state_v, [(state_v, out_state)]),
        (grad, grad_v, [(grad_v, out_grad)]),
        (total, total_v, [(total_v.at[0:3], out_1), (total_v.at[3], out_2), (total_v.at[4], out_3)]),
    ]):
        loads.append(pltpu.make_async_copy(src, held, in_sem.at[i]))
        stores.append([pltpu.make_async_copy(p, q, out_sem.at[i + k]) for k, (p, q) in enumerate(parts)])
    for load in loads:
        load.start()
    for load, parts in zip(loads, stores):
        load.wait()
        for store in parts:
            store.start()
    for parts in stores:
        for store in parts:
            store.wait()


def results(state, grad, edges, total):
    hbm = pl.BlockSpec(memory_space=pltpu.HBM)
    dma = pltpu.SemaphoreType.DMA
    return pl.pallas_call(
        results_kernel,
        out_shape=(
            jax.ShapeDtypeStruct(state.shape, BF16),
            jax.ShapeDtypeStruct(grad.shape, BF16),
            jax.ShapeDtypeStruct(edges.shape, BF16),
            jax.ShapeDtypeStruct((3, 8, D), F32),
            jax.ShapeDtypeStruct((8, D), F32),
            jax.ShapeDtypeStruct((8, D), F32),
        ),
        in_specs=[hbm] * 4,
        out_specs=(hbm,) * 6,
        scratch_shapes=[
            pltpu.VMEM(state.shape, BF16), pltpu.VMEM(grad.shape, BF16),
            pltpu.VMEM(edges.shape, BF16), pltpu.VMEM(total.shape, F32),
            dma((7,)), dma((9,)),
        ],
        compiler_params=pltpu.CompilerParams(vmem_limit_bytes=VMEM_MIB << 20),
        name="results",
    )(state, grad, edges, total)


def body(node_state, edge_state, cotangent, w_first, w_second, w_third,
         pair_near, pair_far, send_fsdp, send_dom):
    new_state, grad_state, grad_edges, total = layer(
        pair_near, pair_far, send_fsdp.reshape(2), send_dom.reshape(2), w_first, w_second, w_third,
        node_state.reshape(NBD, BLOCK, D), cotangent.reshape(NBD, BLOCK, D), edge_state,
    )
    new_state, grad_state, grad_edges, g1, g2, g3 = results(new_state, grad_state, grad_edges, total)
    return (
        new_state.reshape(NBD * BLOCK, D),
        grad_state.reshape(NBD * BLOCK, D),
        grad_edges,
        g1.reshape(24, D),
        g2,
        g3,
    )


def solution(mesh):
    cells = P(("dom", "fsdp"), None)
    rows = P("fsdp", None)
    flat = P(("dom", "fsdp"))
    lists = P(("dom", "fsdp"), None, None)
    return jax.shard_map(
        body,
        mesh=mesh,
        in_specs=(cells, cells, cells, rows, rows, rows, flat, flat, lists, lists),
        out_specs=(cells, cells, cells, rows, rows, rows),
        check_vma=False,
    )
```

```python
import jax
import jax.numpy as jnp
from jax import lax
from jax.experimental import pallas as pl
from jax.experimental.pallas import tpu as pltpu
from jax.sharding import PartitionSpec as P

BLOCK = 128
D = 256
NBD = 6
NH = 4
NEXT = NBD + NH
PAIRS = 16
NX, NY, NZ = 4, 4, 8
NZH = NZ // 2
UNITS = 5
CHUNK = 4
UNROLL = True
VMEM_MIB = 58
LENT_CHUNK = 2
MESH = pl.DeviceIdType.MESH
F32, BF16 = jnp.float32, jnp.bfloat16


def place():
    a = lax.axis_index("dom")
    f = lax.axis_index("fsdp")
    return a, f, a // 2, lax.rem(a, 2), f // NZ, lax.rem(f, NZ)


def halo_peers(a, f):
    nd, nf = 2 * NX, NY * NZ
    return (
        (a, lax.rem(f + nf - 1, nf)),
        (a, lax.rem(f + 1, nf)),
        (lax.rem(a + nd - 1, nd), f),
        (lax.rem(a + 1, nd), f),
    )


def signal_all(peers):
    barrier = pltpu.get_barrier_semaphore()
    for peer in peers:
        pl.semaphore_signal(barrier, inc=1, device_id=peer, device_id_type=MESH)


def wait_all(count):
    pl.semaphore_wait(pltpu.get_barrier_semaphore(), count)


def remote(src, dst, send, recv, peer):
    return pltpu.make_async_remote_copy(
        src_ref=src, dst_ref=dst, send_sem=send, recv_sem=recv,
        device_id=peer, device_id_type=MESH,
    )


def mm(p, q):
    return jnp.dot(p, q, preferred_element_type=F32)


def mm_t(p, q):
    return lax.dot_general(p, q, (((1,), (1,)), ((), ())), preferred_element_type=F32)


def t_mm(p, q):
    return lax.dot_general(p, q, (((0,), (0,)), ((), ())), preferred_element_type=F32)


def act_slope(half):
    up = 1.0 + jnp.tanh(half)
    act = half * up
    return act, up + act * (2.0 - up)


def layer_kernel(
    near_hbm, far_hbm, sf_hbm, sd_hbm, w1_hbm, w2_hbm, w3_hbm, node_hbm, cot_hbm, edge_hbm,
    state_out, grad_out, edge_out, pieces_out, order_out,
    near_in, far_in, sf, sd, order, near, far, chain, last, w1s, w2s, w3s, node, cot, edge_in, edge, lend, wall, halo,
    w1, w1h, w2h, w3, w3h, left, right, ctab, tsum, ysum, a1, d1, gg, sg, dd, ef,
    first, acc_2, acc_3, grads, back, state_part, grad_part,
    got, sibbuf, q, ybuf, r, zbuf, fin, new_state, grad_state, ge,
    os, ls, zs, zr, ys, yr, ss, sr, hs, hr, bs, br, s0, r0, y2s, y2r, z2s, z2r, fs, fr,
):
    a, f, x, c, y, z = place()
    zh, zc = z // 2, lax.rem(z, 2)
    sib = (a + 1 - 2 * c, f)
    ypeers = [(a, lax.rem(y + d, NY) * NZ + z) for d in range(1, NY)]
    zpeers = [(a, y * NZ + lax.rem(z + d, NZ)) for d in range(1, NZ)]
    dpeers = [(lax.rem(a + d, 2 * NX), f) for d in range(1, 2 * NX)]
    hpeers = halo_peers(a, f)
    everyone = zpeers + ypeers + dpeers + list(hpeers)
    signal_all(everyone)

    loads = [
        pltpu.make_async_copy(src, dst, ls.at[i])
        for i, (src, dst) in enumerate((
            (w1_hbm, w1s), (w2_hbm, w2s), (w3_hbm, w3s), (sf_hbm, sf), (sd_hbm, sd),
            (node_hbm, node), (cot_hbm, cot), (near_hbm, near_in), (far_hbm, far_in), (edge_hbm, edge_in),
        ))
    ]
    for copy in loads:
        copy.start()
    for copy in loads[:3]:
        copy.wait()

    @pl.when(zc == c)
    def _():
        wall[y, zh, c, 0:3] = w1s[...].astype(F32).reshape(3, 8, D).astype(BF16)
        wall[y, zh, c, 3] = w2s[...]
        wall[y, zh, c, 4] = w3s[...]

    for copy in loads[3:7]:
        copy.wait()
    for s in range(2):
        b = sf[s]
        lend[s, 0] = node[b]
        lend[s, 1] = cot[b]
        b = sd[s]
        lend[2 + s, 0] = node[b]
        lend[2 + s, 1] = cot[b]
    wait_all(len(everyone))

    halos = [
        remote(lend.at[s], halo.at[s ^ 1], hs.at[s], hr.at[s ^ 1], hpeers[s])
        for s in range(NH)
    ]
    zcopies = [
        remote(wall.at[y, zh, c], wall.at[y, zh, c], zs.at[d], zr.at[zh], zpeers[d])
        for d in (3, 2, 4, 1, 5, 0, 6)
    ]

    @pl.when(zc == c)
    def _():
        for copy in zcopies:
            copy.start()

    halos[2].start()
    halos[3].start()

    loads[7].wait()
    loads[8].wait()
    count, place_of = jnp.int32(0), []
    for p in range(PAIRS):
        entry = far_in[p]
        own_place = count + jnp.where(count < LENT_CHUNK * CHUNK, 0, CHUNK)
        place_of.append(jnp.where(entry < NBD, own_place, entry + (LENT_CHUNK * CHUNK - NBD)))
        count = count + jnp.where(entry < NBD, 1, 0)

    def arrange(i, carry):
        pair, near_i, far_i = jnp.int32(0), near_in[0], far_in[0]
        for p in range(1, PAIRS):
            here = place_of[p] == i
            pair = jnp.where(here, p, pair)
            near_i = jnp.where(here, near_in[p], near_i)
            far_i = jnp.where(here, far_in[p], far_i)
        order[i] = pair
        near[i] = near_i
        far[i] = far_i
        return carry

    lax.fori_loop(0, PAIRS, arrange, 0)

    keys = [(near, far)[h % 2][h // 2] for h in range(2 * PAIRS)]

    def link(h, carry):
        p = h // 2
        key = jnp.where(lax.rem(h, 2) == 0, near[p], far[p])
        before = jnp.int32(2 * PAIRS)
        for g in range(2 * PAIRS):
            before = jnp.where((keys[g] == key) & (g < h), g, before)
        chain[h] = before
        return carry

    lax.fori_loop(0, 2 * PAIRS, link, 0)

    def end(b, carry):
        where = jnp.int32(2 * PAIRS)
        for g in range(2 * PAIRS):
            where = jnp.where(keys[g] == b, g, where)
        last[b] = where
        return carry

    lax.fori_loop(0, NEXT, end, 0)

    sent = []

    def pass_on(yy, h, slot, along_y):
        part = wall.at[yy, h, c]
        if along_y:
            for d, peer in enumerate(ypeers):
                copy = remote(part, part, ys.at[slot, d], yr.at[y, h], peer)
                copy.start()
                sent.append(copy)
        copy = remote(part, part, ss.at[slot], sr.at[yy, h], sib)
        copy.start()
        sent.append(copy)

    for i, d in enumerate((0, 1, 3, 2)):
        h = lax.rem(zh + d, NZH)

        @pl.when(2 * h + c != z)
        def _():
            part = wall.at[y, h, c]
            remote(part, part, zs.at[0], zr.at[h], sib).wait_recv()

        pass_on(y, h, i, True)

    tsum[2 * PAIRS] = jnp.zeros((BLOCK, D), F32)
    ysum[0, 2 * PAIRS] = jnp.zeros((BLOCK, D), F32)
    ysum[1, 2 * PAIRS] = jnp.zeros((BLOCK, D), F32)
    ctab[0:NBD] = cot[...]

    for i, d in enumerate((0, 1, 3, 2)):
        h = lax.rem(zh + d, NZH)
        for e in (1, 3, 2):
            yy = lax.rem(y + e, NY)
            part = wall.at[yy, h, c]
            remote(part, part, ys.at[0, 0], yr.at[yy, h], sib).wait_recv()
            pass_on(yy, h, 4 * e + i, False)
    halos[0].start()
    halos[1].start()
    loads[9].wait()
    rows = CHUNK * BLOCK
    direct = [slice(j * BLOCK, (j + 1) * BLOCK) for j in range(CHUNK)]
    mirror = [slice(rows + j * BLOCK, rows + (j + 1) * BLOCK) for j in range(CHUNK)]
    own_rows = NBD * BLOCK
    for yy in range(NY):
        for h in range(NZH):
            part = wall.at[yy, h, 1 - c]
            remote(part, part, ss.at[0], sr.at[yy, h], sib).wait_recv()

    packed = wall[...].reshape(NY * NZ, UNITS, 8, D).astype(F32)
    flat = packed[:, 0:3].reshape(3 * D, D)
    w1[...] = flat.astype(BF16)
    w1h[...] = (0.5 * flat).astype(BF16)
    w2h[...] = (0.5 * packed[:, 3].reshape(D, D)).astype(BF16)
    third = packed[:, 4].reshape(D, D)
    w3[...] = third.astype(BF16)
    w3h[...] = (0.5 * third).astype(BF16)
    own = node[...].reshape(own_rows, D)
    for table, cols in ((left, 0), (right, D)):
        table[0:NBD] = mm(own, w1h[cols:cols + D]).reshape(NBD, BLOCK, D)

    def part_of(ref, steps):
        return ref[0:steps].reshape(-1, D)

    def chunk(i, carry):
        pairs = [i * CHUNK + j for j in range(CHUNK)]
        ends = [(near[p], far[p]) for p in pairs]
        links = [(2 * p, chain[2 * p], chain[2 * p + 1]) for p in pairs]
        span = pl.ds(pl.multiple_of(i * rows, rows), rows)
        for j, p in enumerate(pairs):
            edge[pl.ds(pl.multiple_of(p * BLOCK, BLOCK), BLOCK)] = edge_in[order[p]]
        edge_part = mm(edge[span], w1h[2 * D:])
        for j, (n, m) in enumerate(ends):
            gg[i, direct[j]] = (ctab[n].astype(F32) - ctab[m].astype(F32)).astype(BF16)
            for where, p, k in ((direct[j], n, m), (mirror[j], m, n)):
                act, slope = act_slope(left[p] + right[k] + edge_part[direct[j]])
                a1[i, where] = act.astype(BF16)
                d1[where] = slope
        second = mm(a1[i], w2h[...])
        back_3 = mm_t(gg[i], w3h[...])
        for j, (h, before_n, before_m) in enumerate(links):
            act_f, slope_f = act_slope(second[direct[j]])
            act_m, slope_m = act_slope(second[mirror[j]])
            diff = act_f - act_m
            dd[i, direct[j]] = diff.astype(BF16)
            tsum[h] = tsum[before_n] + diff
            tsum[h + 1] = tsum[before_m] - diff
            sg[i, direct[j]] = (back_3[direct[j]] * slope_f).astype(BF16)
            sg[i, mirror[j]] = (-back_3[direct[j]] * slope_m).astype(BF16)
        first_back = mm_t(sg[i], w2h[...])
        for j, (h, before_n, before_m) in enumerate(links):
            part_f = first_back[direct[j]] * d1[direct[j]]
            part_m = first_back[mirror[j]] * d1[mirror[j]]
            ef[i, direct[j]] = (part_f + part_m).astype(BF16)
            ysum[0, h] = ysum[0, before_n] + part_f
            ysum[0, h + 1] = ysum[0, before_m] + part_m
            ysum[1, h] = ysum[1, before_n] + part_m
            ysum[1, h + 1] = ysum[1, before_m] + part_f
        ge[span] = mm_t(ef[i], w1[2 * D:]).astype(BF16)
        return carry

    final = PAIRS // CHUNK - 1
    lax.fori_loop(0, LENT_CHUNK, chunk, 0, unroll=UNROLL)

    for s in range(NH):
        halos[s].wait_recv()
    ctab[NBD:] = halo[:, 1]
    lent = halo[:, 0].reshape(NH * BLOCK, D)
    for table, cols in ((left, 0), (right, D)):
        table[NBD:] = mm(lent, w1h[cols:cols + D]).reshape(NH, BLOCK, D)
    chunk(LENT_CHUNK, 0)

    wa, wb = w1[0:D], w1[D:2 * D]
    lent_ends = [2 * (LENT_CHUNK * CHUNK + k) + 1 for k in range(NH)]

    def lent_sum(ref):
        return jnp.concatenate([ref[h].astype(BF16) for h in lent_ends], 0)

    lent_flux = mm(lent_sum(tsum), w3[...])
    lent_grad = mm_t(lent_sum(ysum.at[0]), wa) + mm_t(lent_sum(ysum.at[1]), wb)
    back[:, 0] = lent_flux.astype(BF16).reshape(NH, BLOCK, D)
    back[:, 1] = lent_grad.astype(BF16).reshape(NH, BLOCK, D)
    backs = [
        remote(back.at[s], got.at[s ^ 1], bs.at[s], br.at[s ^ 1], hpeers[s])
        for s in range(NH)
    ]
    for copy in backs:
        copy.start()

    lax.fori_loop(LENT_CHUNK + 1, PAIRS // CHUNK, chunk, 0, unroll=UNROLL)
    first[2 * D:] = t_mm(edge[0:final * rows], part_of(ef, final))
    acc_2[...] = t_mm(part_of(a1, final), part_of(sg, final))
    acc_3[...] = t_mm(part_of(dd, final), part_of(gg, final))
    stores = [
        pltpu.make_async_copy(src, dst, os.at[i])
        for i, (src, dst) in enumerate((
            (ge, edge_out), (new_state, state_out), (grad_state, grad_out),
        ))
    ]
    stores[0].start()
    order_store = pltpu.make_async_copy(order, order_out, os.at[4])
    order_store.start()

    ends = [last[b] for b in range(NEXT)]

    def gathered(pick):
        return jnp.concatenate([pick(h).astype(BF16) for h in ends], 0)

    ts = gathered(lambda h: tsum[h])
    ya = gathered(lambda h: ysum[0, h])
    yb = gathered(lambda h: ysum[1, h])

    pieces = (slice(3, 5), slice(0, 3))

    def to_sibling(k):
        copy = remote(grads.at[:, :, 1 - c, pieces[k]], sibbuf.at[:, :, pieces[k]], s0.at[k], r0.at[k], sib)
        copy.start()
        return copy

    grads[:, :, :, 3] = (acc_2[...] + t_mm(a1[final], sg[final])).reshape(NY, NZH, 2, 8, D).astype(BF16)
    grads[:, :, :, 4] = (acc_3[...] + t_mm(dd[final], gg[final])).reshape(NY, NZH, 2, 8, D).astype(BF16)
    cores = [to_sibling(0)]
    first[0:D] = t_mm(own, ya[:own_rows]) + t_mm(lent, ya[own_rows:])
    first[D:2 * D] = t_mm(own, yb[:own_rows]) + t_mm(lent, yb[own_rows:])
    first[2 * D:] += t_mm(edge[final * rows:], ef[final])
    grads[:, :, :, 0:3] = first[...].reshape(NY, NZH, 2, 3, 8, D).astype(BF16)
    cores.append(to_sibling(1))

    ycopies = []
    for k, piece in enumerate(pieces):
        cores[k].wait_recv()
        q[:, :, piece] = (grads[:, :, c, piece].astype(F32) + sibbuf[:, :, piece].astype(F32)).astype(BF16)
        for d, peer in enumerate(ypeers):
            yy = lax.rem(y + d + 1, NY)
            copy = remote(q.at[yy, :, piece], ybuf.at[d, :, piece], y2s.at[k, d], y2r.at[k, d], peer)
            copy.start()
            ycopies.append(copy)

    flux = mm(ts[:own_rows], w3[...]).reshape(NBD, BLOCK, D)
    state_part[...] = node[...].astype(F32) + flux
    node_grad = mm_t(ya[:own_rows], wa) + mm_t(yb[:own_rows], wb)
    grad_part[...] = cot[...].astype(F32) + node_grad.reshape(NBD, BLOCK, D)

    value = q[y].astype(F32)
    for copy in ycopies:
        copy.wait_recv()
    for d in range(NY - 1):
        value = value + ybuf[d].astype(F32)
    r[...] = value.astype(BF16)

    rcopies = []
    for k, d in enumerate((2, 1, 3, 0)):
        h = lax.rem(zh + d, NZH)
        copy = remote(r.at[h], zbuf.at[z], z2s.at[k], z2r.at[z], (a, y * NZ + 2 * h + c))
        rcopies.append((h, copy))

        @pl.when(2 * h + c != z)
        def _():
            copy.start()

    for copy in backs:
        copy.wait_recv()
    owner = (sf[0], sf[1], sd[0], sd[1])

    def settle(k, part, out):
        for b in range(NBD):
            value = part[b]
            for s in range(NH):
                value = value + jnp.where(owner[s] == b, got[s, k].astype(F32), 0.0)
            out[b] = value.astype(BF16)

    settle(0, state_part, new_state)
    stores[1].start()
    settle(1, grad_part, grad_state)
    stores[2].start()

    fcopies = [
        remote(fin, pieces_out.at[x], fs.at[d], fr.at[x], dpeers[d]) for d in (3, 4, 2, 5, 1, 6, 0)
    ]

    @pl.when(zc == c)
    def _():
        acc = r[zh].astype(F32)
        for d in (1, 7, 2, 6, 3, 5, 4):
            zz = lax.rem(z + d, NZ)
            remote(r.at[0], zbuf.at[zz], z2s.at[0], z2r.at[zz], sib).wait_recv()
            acc = acc + zbuf[zz].astype(F32)
        fin[...] = acc.astype(BF16)
        for copy in fcopies:
            copy.start()
        own_piece = pltpu.make_async_copy(fin, pieces_out.at[x], os.at[3])
        own_piece.start()
        for copy in fcopies:
            copy.wait_send()
        own_piece.wait()

    @pl.when(zc != c)
    def _():
        remote(fin, pieces_out.at[x], fs.at[0], fr.at[x], sib).wait_recv()

    for d in range(1, NX):
        xx = lax.rem(x + d, NX)
        remote(fin, pieces_out.at[xx], fs.at[0], fr.at[xx], sib).wait_recv()

    for h, copy in rcopies:
        @pl.when(2 * h + c != z)
        def _():
            copy.wait_send()

    @pl.when(zc == c)
    def _():
        for copy in zcopies:
            copy.wait_send()

    for copy in sent + halos + backs + cores + ycopies:
        copy.wait_send()
    for copy in stores + [order_store]:
        copy.wait()


def layer(near, far, sf, sd, w1, w2, w3, node, cot, edge):
    hbm = pl.BlockSpec(memory_space=pltpu.HBM)
    dma = pltpu.SemaphoreType.DMA
    steps, rows = PAIRS // CHUNK, CHUNK * BLOCK
    shard = (UNITS, 8, D)

    def smem(count):
        return pltpu.SMEM((count,), jnp.int32)

    def bf(*shape):
        return pltpu.VMEM(shape, BF16)

    def f32(*shape):
        return pltpu.VMEM(shape, F32)

    lent = bf(NH, 2, BLOCK, D)
    blocks = f32(NBD, BLOCK, D)
    return pl.pallas_call(
        layer_kernel,
        out_shape=(
            jax.ShapeDtypeStruct(node.shape, BF16),
            jax.ShapeDtypeStruct(cot.shape, BF16),
            jax.ShapeDtypeStruct((PAIRS * BLOCK, D), BF16),
            jax.ShapeDtypeStruct((NX, *shard), BF16),
            jax.ShapeDtypeStruct((PAIRS,), jnp.int32),
        ),
        in_specs=[hbm] * 10,
        out_specs=(hbm,) * 5,
        scratch_shapes=[
            smem(PAIRS), smem(PAIRS), smem(2), smem(2), smem(PAIRS), smem(PAIRS), smem(PAIRS), smem(2 * PAIRS), smem(NEXT),
            bf(*w1.shape), bf(*w2.shape), bf(*w3.shape), bf(*node.shape), bf(*cot.shape), bf(*edge.shape), bf(PAIRS * BLOCK, D),
            lent, bf(NY, NZH, 2, *shard), lent,
            bf(3 * D, D), bf(3 * D, D), bf(D, D), bf(D, D), bf(D, D),
            f32(NEXT, BLOCK, D), f32(NEXT, BLOCK, D), bf(NEXT, BLOCK, D),
            f32(2 * PAIRS + 1, BLOCK, D), f32(2, 2 * PAIRS + 1, BLOCK, D),
            bf(steps, 2 * rows, D), f32(2 * rows, D), bf(steps, rows, D), bf(steps, 2 * rows, D),
            bf(steps, rows, D), bf(steps, rows, D),
            f32(3 * D, D), f32(D, D), f32(D, D), bf(NY, NZH, 2, *shard), lent, blocks, blocks,
            lent, bf(NY, NZH, *shard), bf(NY, NZH, *shard), bf(NY - 1, NZH, *shard), bf(NZH, *shard),
            bf(NZ, *shard), bf(*shard),
            bf(*node.shape), bf(*cot.shape), bf(PAIRS * BLOCK, D),
            dma((5,)), dma((10,)), dma((NZ - 1,)), dma((NZH,)), dma((NZH, NY - 1)), dma((NY, NZH)),
            dma((NY * NZH,)), dma((NY, NZH)), dma((NH,)), dma((NH,)), dma((NH,)), dma((NH,)),
            dma((2,)), dma((2,)), dma((2, NY - 1)), dma((2, NY - 1)),
            dma((NZH,)), dma((NZ,)), dma((2 * NX - 1,)), dma((NX,)),
        ],
        compiler_params=pltpu.CompilerParams(
            collective_id=0, has_side_effects=True, vmem_limit_bytes=VMEM_MIB << 20
        ),
        name="layer",
    )(near, far, sf, sd, w1, w2, w3, node, cot, edge)


def results_kernel(
    order_hbm, state, grad, edges, total, out_state, out_grad, out_edges, out_1, out_2, out_3,
    order, state_v, grad_v, edges_v, sum_v, total_v, order_sem, in_sem, out_sem,
):
    order_copy = pltpu.make_async_copy(order_hbm, order, order_sem)
    order_copy.start()
    quarter = CHUNK * BLOCK
    spans = [pl.ds(i * quarter, quarter) for i in range(PAIRS // CHUNK)]
    loads = [
        pltpu.make_async_copy(src, held, in_sem.at[i])
        for i, (src, held) in enumerate(
            [(edges.at[s], edges_v.at[s]) for s in spans]
            + [(state, state_v), (grad, grad_v), (total, sum_v)]
        )
    ]
    for load in loads:
        load.start()
    order_copy.wait()
    stores = []

    def store(src, dst):
        copy = pltpu.make_async_copy(src, dst, out_sem.at[len(stores)])
        copy.start()
        stores.append(copy)

    for i in range(PAIRS):
        if i % CHUNK == 0:
            loads[i // CHUNK].wait()
        rows = pl.ds(pl.multiple_of(order[i] * BLOCK, BLOCK), BLOCK)
        store(edges_v.at[pl.ds(i * BLOCK, BLOCK)], out_edges.at[rows])
    loads[4].wait()
    store(state_v, out_state)
    loads[5].wait()
    store(grad_v, out_grad)
    loads[6].wait()
    total_v[...] = sum((sum_v[i].astype(F32) for i in range(1, NX)), sum_v[0].astype(F32))
    store(total_v.at[0:3], out_1)
    store(total_v.at[3], out_2)
    store(total_v.at[4], out_3)
    for copy in stores:
        copy.wait()


def results(order, state, grad, edges, total):
    hbm = pl.BlockSpec(memory_space=pltpu.HBM)
    dma = pltpu.SemaphoreType.DMA
    return pl.pallas_call(
        results_kernel,
        out_shape=(
            jax.ShapeDtypeStruct(state.shape, BF16),
            jax.ShapeDtypeStruct(grad.shape, BF16),
            jax.ShapeDtypeStruct(edges.shape, BF16),
            jax.ShapeDtypeStruct((3, 8, D), F32),
            jax.ShapeDtypeStruct((8, D), F32),
            jax.ShapeDtypeStruct((8, D), F32),
        ),
        in_specs=[hbm] * 5,
        out_specs=(hbm,) * 6,
        scratch_shapes=[
            pltpu.SMEM((PAIRS,), jnp.int32),
            pltpu.VMEM(state.shape, BF16), pltpu.VMEM(grad.shape, BF16),
            pltpu.VMEM(edges.shape, BF16), pltpu.VMEM(total.shape, BF16), pltpu.VMEM(total.shape[1:], F32),
            dma, dma((7,)), dma((PAIRS + 5,)),
        ],
        compiler_params=pltpu.CompilerParams(vmem_limit_bytes=VMEM_MIB << 20),
        name="results",
    )(order, state, grad, edges, total)


def body(node_state, edge_state, cotangent, w_first, w_second, w_third,
         pair_near, pair_far, send_fsdp, send_dom):
    new_state, grad_state, grad_edges, total, order = layer(
        pair_near, pair_far, send_fsdp.reshape(2), send_dom.reshape(2), w_first, w_second, w_third,
        node_state.reshape(NBD, BLOCK, D), cotangent.reshape(NBD, BLOCK, D),
        edge_state.reshape(PAIRS, BLOCK, D),
    )
    new_state, grad_state, grad_edges, g1, g2, g3 = results(
        order, new_state, grad_state, grad_edges, total
    )
    return (
        new_state.reshape(NBD * BLOCK, D),
        grad_state.reshape(NBD * BLOCK, D),
        grad_edges,
        g1.reshape(24, D),
        g2,
        g3,
    )


def solution(mesh):
    cells = P(("dom", "fsdp"), None)
    rows = P("fsdp", None)
    flat = P(("dom", "fsdp"))
    lists = P(("dom", "fsdp"), None, None)
    return jax.shard_map(
        body,
        mesh=mesh,
        in_specs=(cells, cells, cells, rows, rows, rows, flat, flat, lists, lists),
        out_specs=(cells, cells, cells, rows, rows, rows),
        check_vma=False,
    )
```

```python
import jax
import jax.numpy as jnp
from jax import lax
from jax.experimental import pallas as pl
from jax.experimental.pallas import tpu as pltpu
from jax.sharding import PartitionSpec as P

BLOCK = 128
D = 256
NBD = 6
NH = 4
NEXT = NBD + NH
PAIRS = 16
NX, NY, NZ = 4, 4, 8
NZH = NZ // 2
UNITS = 5
CHUNK = 4
UNROLL = True
VMEM_MIB = 58
LENT_CHUNK = 2
MESH = pl.DeviceIdType.MESH
F32, BF16 = jnp.float32, jnp.bfloat16


def place():
    a = lax.axis_index("dom")
    f = lax.axis_index("fsdp")
    return a, f, a // 2, lax.rem(a, 2), f // NZ, lax.rem(f, NZ)


def halo_peers(a, f):
    nd, nf = 2 * NX, NY * NZ
    return (
        (a, lax.rem(f + nf - 1, nf)),
        (a, lax.rem(f + 1, nf)),
        (lax.rem(a + nd - 1, nd), f),
        (lax.rem(a + 1, nd), f),
    )


def signal_all(peers):
    barrier = pltpu.get_barrier_semaphore()
    for peer in peers:
        pl.semaphore_signal(barrier, inc=1, device_id=peer, device_id_type=MESH)


def wait_all(count):
    pl.semaphore_wait(pltpu.get_barrier_semaphore(), count)


def remote(src, dst, send, recv, peer):
    return pltpu.make_async_remote_copy(
        src_ref=src, dst_ref=dst, send_sem=send, recv_sem=recv,
        device_id=peer, device_id_type=MESH,
    )


def mm(p, q):
    return jnp.dot(p, q, preferred_element_type=F32)


def mm_t(p, q):
    return lax.dot_general(p, q, (((1,), (1,)), ((), ())), preferred_element_type=F32)


def t_mm(p, q):
    return lax.dot_general(p, q, (((0,), (0,)), ((), ())), preferred_element_type=F32)


def act_slope(half):
    up = 1.0 + jnp.tanh(half)
    act = half * up
    return act, up + act * (2.0 - up)


def layer_kernel(
    near_hbm, far_hbm, sf_hbm, sd_hbm, w1_hbm, w2_hbm, w3_hbm, node_hbm, cot_hbm, edge_hbm,
    state_out, grad_out, edge_out, pieces_out, order_out,
    near_in, far_in, sf, sd, order, near, far, chain, last, w1s, w2s, w3s, node, cot, edge_in, edge, lend, wall, halo,
    w1, w1h, w2h, w3, w3h, left, right, ctab, tsum, ysum, a1, d1, gg, sg, dd, ef,
    first, acc_2, acc_3, grads, back, state_part, grad_part,
    got, sibbuf, q, ybuf, r, zbuf, fin, new_state, grad_state, ge,
    os, ls, zs, zr, ys, yr, ss, sr, hs, hr, bs, br, s0, r0, y2s, y2r, z2s, z2r, fs, fr,
):
    a, f, x, c, y, z = place()
    zh, zc = z // 2, lax.rem(z, 2)
    sib = (a + 1 - 2 * c, f)
    ypeers = [(a, lax.rem(y + d, NY) * NZ + z) for d in range(1, NY)]
    zpeers = [(a, y * NZ + lax.rem(z + d, NZ)) for d in range(1, NZ)]
    dpeers = [(lax.rem(a + d, 2 * NX), f) for d in range(1, 2 * NX)]
    hpeers = halo_peers(a, f)
    everyone = [zpeers[d] for d in (3, 2, 4, 1, 5, 0, 6)] + ypeers + dpeers + list(hpeers[:2])
    signal_all(everyone)

    loads = [
        pltpu.make_async_copy(src, dst, ls.at[i])
        for i, (src, dst) in enumerate((
            (w1_hbm, w1s), (w2_hbm, w2s), (w3_hbm, w3s), (sf_hbm, sf), (sd_hbm, sd),
            (node_hbm, node), (cot_hbm, cot), (near_hbm, near_in), (far_hbm, far_in), (edge_hbm, edge_in),
        ))
    ]
    for copy in loads:
        copy.start()
    for copy in loads[:3]:
        copy.wait()

    @pl.when(zc == c)
    def _():
        wall[y, zh, c, 0:3] = w1s[...].astype(F32).reshape(3, 8, D).astype(BF16)
        wall[y, zh, c, 3] = w2s[...]
        wall[y, zh, c, 4] = w3s[...]

    for copy in loads[3:7]:
        copy.wait()
    for s in range(2):
        b = sf[s]
        lend[s, 0] = node[b]
        lend[s, 1] = cot[b]
        b = sd[s]
        lend[2 + s, 0] = node[b]
        lend[2 + s, 1] = cot[b]
    wait_all(len(everyone))

    halos = [
        remote(lend.at[s], halo.at[s ^ 1], hs.at[s], hr.at[s ^ 1], hpeers[s])
        for s in range(NH)
    ]
    zcopies = [
        remote(wall.at[y, zh, c], wall.at[y, zh, c], zs.at[d], zr.at[zh], zpeers[d])
        for d in (3, 2, 4, 1, 5, 0, 6)
    ]

    @pl.when(zc == c)
    def _():
        for copy in zcopies:
            copy.start()

    halos[2].start()
    halos[3].start()

    loads[7].wait()
    loads[8].wait()
    count, place_of = jnp.int32(0), []
    for p in range(PAIRS):
        entry = far_in[p]
        own_place = count + jnp.where(count < LENT_CHUNK * CHUNK, 0, CHUNK)
        place_of.append(jnp.where(entry < NBD, own_place, entry + (LENT_CHUNK * CHUNK - NBD)))
        count = count + jnp.where(entry < NBD, 1, 0)

    def arrange(i, carry):
        pair, near_i, far_i = jnp.int32(0), near_in[0], far_in[0]
        for p in range(1, PAIRS):
            here = place_of[p] == i
            pair = jnp.where(here, p, pair)
            near_i = jnp.where(here, near_in[p], near_i)
            far_i = jnp.where(here, far_in[p], far_i)
        order[i] = pair
        near[i] = near_i
        far[i] = far_i
        return carry

    lax.fori_loop(0, PAIRS, arrange, 0)

    keys = [(near, far)[h % 2][h // 2] for h in range(2 * PAIRS)]

    def link(h, carry):
        p = h // 2
        key = jnp.where(lax.rem(h, 2) == 0, near[p], far[p])
        before = jnp.int32(2 * PAIRS)
        for g in range(2 * PAIRS):
            before = jnp.where((keys[g] == key) & (g < h), g, before)
        chain[h] = before
        return carry

    lax.fori_loop(0, 2 * PAIRS, link, 0)

    def end(b, carry):
        where = jnp.int32(2 * PAIRS)
        for g in range(2 * PAIRS):
            where = jnp.where(keys[g] == b, g, where)
        last[b] = where
        return carry

    lax.fori_loop(0, NEXT, end, 0)

    sent = []

    def pass_on(yy, h, slot, along_y):
        part = wall.at[yy, h, c]
        if along_y:
            for d, peer in enumerate(ypeers):
                copy = remote(part, part, ys.at[slot, d], yr.at[y, h], peer)
                copy.start()
                sent.append(copy)
        copy = remote(part, part, ss.at[slot], sr.at[yy, h], sib)
        copy.start()
        sent.append(copy)

    for i, d in enumerate((0, 1, 3, 2)):
        h = lax.rem(zh + d, NZH)

        @pl.when(2 * h + c != z)
        def _():
            part = wall.at[y, h, c]
            remote(part, part, zs.at[0], zr.at[h], sib).wait_recv()

        pass_on(y, h, i, True)

    tsum[2 * PAIRS] = jnp.zeros((BLOCK, D), F32)
    ysum[0, 2 * PAIRS] = jnp.zeros((BLOCK, D), F32)
    ysum[1, 2 * PAIRS] = jnp.zeros((BLOCK, D), F32)
    ctab[0:NBD] = cot[...]

    for i, d in enumerate((0, 1, 3, 2)):
        h = lax.rem(zh + d, NZH)
        for e in (1, 3, 2):
            yy = lax.rem(y + e, NY)
            part = wall.at[yy, h, c]
            remote(part, part, ys.at[0, 0], yr.at[yy, h], sib).wait_recv()
            pass_on(yy, h, 4 * e + i, False)
    halos[0].start()
    halos[1].start()
    loads[9].wait()
    rows = CHUNK * BLOCK
    direct = [slice(j * BLOCK, (j + 1) * BLOCK) for j in range(CHUNK)]
    mirror = [slice(rows + j * BLOCK, rows + (j + 1) * BLOCK) for j in range(CHUNK)]
    own_rows = NBD * BLOCK
    for yy in range(NY):
        for h in range(NZH):
            part = wall.at[yy, h, 1 - c]
            remote(part, part, ss.at[0], sr.at[yy, h], sib).wait_recv()

    packed = wall[...].reshape(NY * NZ, UNITS, 8, D).astype(F32)
    flat = packed[:, 0:3].reshape(3 * D, D)
    w1[...] = flat.astype(BF16)
    w1h[...] = (0.5 * flat).astype(BF16)
    w2h[...] = (0.5 * packed[:, 3].reshape(D, D)).astype(BF16)
    third = packed[:, 4].reshape(D, D)
    w3[...] = third.astype(BF16)
    w3h[...] = (0.5 * third).astype(BF16)
    own = node[...].reshape(own_rows, D)
    for table, cols in ((left, 0), (right, D)):
        table[0:NBD] = mm(own, w1h[cols:cols + D]).reshape(NBD, BLOCK, D)

    def part_of(ref, steps):
        return ref[0:steps].reshape(-1, D)

    def chunk(i, carry):
        pairs = [i * CHUNK + j for j in range(CHUNK)]
        ends = [(near[p], far[p]) for p in pairs]
        links = [(2 * p, chain[2 * p], chain[2 * p + 1]) for p in pairs]
        span = pl.ds(pl.multiple_of(i * rows, rows), rows)
        for j, p in enumerate(pairs):
            edge[pl.ds(pl.multiple_of(p * BLOCK, BLOCK), BLOCK)] = edge_in[order[p]]
        edge_part = mm(edge[span], w1h[2 * D:])
        for j, (n, m) in enumerate(ends):
            gg[i, direct[j]] = (ctab[n].astype(F32) - ctab[m].astype(F32)).astype(BF16)
            for where, p, k in ((direct[j], n, m), (mirror[j], m, n)):
                act, slope = act_slope(left[p] + right[k] + edge_part[direct[j]])
                a1[i, where] = act.astype(BF16)
                d1[where] = slope
        second = mm(a1[i], w2h[...])
        back_3 = mm_t(gg[i], w3h[...])
        for j, (h, before_n, before_m) in enumerate(links):
            act_f, slope_f = act_slope(second[direct[j]])
            act_m, slope_m = act_slope(second[mirror[j]])
            diff = act_f - act_m
            dd[i, direct[j]] = diff.astype(BF16)
            tsum[h] = tsum[before_n] + diff
            tsum[h + 1] = tsum[before_m] - diff
            sg[i, direct[j]] = (back_3[direct[j]] * slope_f).astype(BF16)
            sg[i, mirror[j]] = (-back_3[direct[j]] * slope_m).astype(BF16)
        first_back = mm_t(sg[i], w2h[...])
        for j, (h, before_n, before_m) in enumerate(links):
            part_f = first_back[direct[j]] * d1[direct[j]]
            part_m = first_back[mirror[j]] * d1[mirror[j]]
            ef[i, direct[j]] = (part_f + part_m).astype(BF16)
            ysum[0, h] = ysum[0, before_n] + part_f
            ysum[0, h + 1] = ysum[0, before_m] + part_m
            ysum[1, h] = ysum[1, before_n] + part_m
            ysum[1, h + 1] = ysum[1, before_m] + part_f
        ge[span] = mm_t(ef[i], w1[2 * D:]).astype(BF16)
        return carry

    final = PAIRS // CHUNK - 1
    lax.fori_loop(0, LENT_CHUNK, chunk, 0, unroll=UNROLL)

    for s in range(NH):
        halos[s].wait_recv()
    ctab[NBD:] = halo[:, 1]
    lent = halo[:, 0].reshape(NH * BLOCK, D)
    for table, cols in ((left, 0), (right, D)):
        table[NBD:] = mm(lent, w1h[cols:cols + D]).reshape(NH, BLOCK, D)
    chunk(LENT_CHUNK, 0)

    wa, wb = w1[0:D], w1[D:2 * D]
    lent_ends = [2 * (LENT_CHUNK * CHUNK + k) + 1 for k in range(NH)]

    def lent_sum(ref):
        return jnp.concatenate([ref[h].astype(BF16) for h in lent_ends], 0)

    lent_flux = mm(lent_sum(tsum), w3[...])
    lent_grad = mm_t(lent_sum(ysum.at[0]), wa) + mm_t(lent_sum(ysum.at[1]), wb)
    back[:, 0] = lent_flux.astype(BF16).reshape(NH, BLOCK, D)
    back[:, 1] = lent_grad.astype(BF16).reshape(NH, BLOCK, D)
    backs = [
        remote(back.at[s], got.at[s ^ 1], bs.at[s], br.at[s ^ 1], hpeers[s])
        for s in range(NH)
    ]
    for copy in backs:
        copy.start()

    lax.fori_loop(LENT_CHUNK + 1, PAIRS // CHUNK, chunk, 0, unroll=UNROLL)
    first[2 * D:] = t_mm(edge[0:final * rows], part_of(ef, final))
    acc_2[...] = t_mm(part_of(a1, final), part_of(sg, final))
    acc_3[...] = t_mm(part_of(dd, final), part_of(gg, final))
    stores = [
        pltpu.make_async_copy(src, dst, os.at[i])
        for i, (src, dst) in enumerate((
            (ge, edge_out), (new_state, state_out), (grad_state, grad_out),
        ))
    ]
    stores[0].start()
    order_store = pltpu.make_async_copy(order, order_out, os.at[4])
    order_store.start()

    ends = [last[b] for b in range(NEXT)]

    def gathered(pick):
        return jnp.concatenate([pick(h).astype(BF16) for h in ends], 0)

    ts = gathered(lambda h: tsum[h])
    ya = gathered(lambda h: ysum[0, h])
    yb = gathered(lambda h: ysum[1, h])

    pieces = (slice(3, 5), slice(0, 3))

    def to_sibling(k):
        copy = remote(grads.at[:, :, 1 - c, pieces[k]], sibbuf.at[:, :, pieces[k]], s0.at[k], r0.at[k], sib)
        copy.start()
        return copy

    grads[:, :, :, 3] = (acc_2[...] + t_mm(a1[final], sg[final])).reshape(NY, NZH, 2, 8, D).astype(BF16)
    grads[:, :, :, 4] = (acc_3[...] + t_mm(dd[final], gg[final])).reshape(NY, NZH, 2, 8, D).astype(BF16)
    cores = [to_sibling(0)]
    first[0:D] = t_mm(own, ya[:own_rows]) + t_mm(lent, ya[own_rows:])
    first[D:2 * D] = t_mm(own, yb[:own_rows]) + t_mm(lent, yb[own_rows:])
    first[2 * D:] += t_mm(edge[final * rows:], ef[final])
    grads[:, :, :, 0:3] = first[...].reshape(NY, NZH, 2, 3, 8, D).astype(BF16)
    cores.append(to_sibling(1))

    ycopies = []
    for k, piece in enumerate(pieces):
        cores[k].wait_recv()
        q[:, :, piece] = (grads[:, :, c, piece].astype(F32) + sibbuf[:, :, piece].astype(F32)).astype(BF16)
        for d, peer in enumerate(ypeers):
            yy = lax.rem(y + d + 1, NY)
            copy = remote(q.at[yy, :, piece], ybuf.at[d, :, piece], y2s.at[k, d], y2r.at[k, d], peer)
            copy.start()
            ycopies.append(copy)

    flux = mm(ts[:own_rows], w3[...]).reshape(NBD, BLOCK, D)
    state_part[...] = node[...].astype(F32) + flux
    node_grad = mm_t(ya[:own_rows], wa) + mm_t(yb[:own_rows], wb)
    grad_part[...] = cot[...].astype(F32) + node_grad.reshape(NBD, BLOCK, D)

    @pl.when(zc == c)
    def _():
        for copy in zcopies:
            copy.wait_send()

    for copy in sent + halos:
        copy.wait_send()
    stores[0].wait()
    order_store.wait()

    value = q[y].astype(F32)
    for copy in ycopies:
        copy.wait_recv()
    for d in range(NY - 1):
        value = value + ybuf[d].astype(F32)
    r[...] = value.astype(BF16)

    rcopies = []
    for k, d in enumerate((2, 1, 3, 0)):
        h = lax.rem(zh + d, NZH)
        copy = remote(r.at[h], zbuf.at[z], z2s.at[k], z2r.at[z], (a, y * NZ + 2 * h + c))
        rcopies.append((h, copy))

        @pl.when(2 * h + c != z)
        def _():
            copy.start()

    for copy in backs:
        copy.wait_recv()
    owner = (sf[0], sf[1], sd[0], sd[1])

    def settle(k, part, out):
        for b in range(NBD):
            value = part[b]
            for s in range(NH):
                value = value + jnp.where(owner[s] == b, got[s, k].astype(F32), 0.0)
            out[b] = value.astype(BF16)

    settle(0, state_part, new_state)
    stores[1].start()
    settle(1, grad_part, grad_state)
    stores[2].start()

    for copy in backs + cores + ycopies:
        copy.wait_send()
    for h, copy in rcopies:
        @pl.when(2 * h + c != z)
        def _():
            copy.wait_send()
    for copy in stores[1:]:
        copy.wait()

    fcopies = [
        remote(fin, pieces_out.at[x], fs.at[d], fr.at[x], dpeers[d]) for d in (3, 4, 2, 5, 1, 6, 0)
    ]

    @pl.when(zc == c)
    def _():
        acc = r[zh].astype(F32)
        for d in (1, 7, 2, 6, 3, 5, 4):
            zz = lax.rem(z + d, NZ)
            remote(r.at[0], zbuf.at[zz], z2s.at[0], z2r.at[zz], sib).wait_recv()
            acc = acc + zbuf[zz].astype(F32)
        fin[...] = acc.astype(BF16)
        for copy in fcopies:
            copy.start()
        own_piece = pltpu.make_async_copy(fin, pieces_out.at[x], os.at[3])
        own_piece.start()
        for copy in fcopies:
            copy.wait_send()
        own_piece.wait()

    @pl.when(zc != c)
    def _():
        remote(fin, pieces_out.at[x], fs.at[0], fr.at[x], sib).wait_recv()

    for d in range(1, NX):
        xx = lax.rem(x + d, NX)
        remote(fin, pieces_out.at[xx], fs.at[0], fr.at[xx], sib).wait_recv()


def layer(near, far, sf, sd, w1, w2, w3, node, cot, edge):
    hbm = pl.BlockSpec(memory_space=pltpu.HBM)
    dma = pltpu.SemaphoreType.DMA
    steps, rows = PAIRS // CHUNK, CHUNK * BLOCK
    shard = (UNITS, 8, D)

    def smem(count):
        return pltpu.SMEM((count,), jnp.int32)

    def bf(*shape):
        return pltpu.VMEM(shape, BF16)

    def f32(*shape):
        return pltpu.VMEM(shape, F32)

    lent = bf(NH, 2, BLOCK, D)
    blocks = f32(NBD, BLOCK, D)
    return pl.pallas_call(
        layer_kernel,
        out_shape=(
            jax.ShapeDtypeStruct(node.shape, BF16),
            jax.ShapeDtypeStruct(cot.shape, BF16),
            jax.ShapeDtypeStruct((PAIRS * BLOCK, D), BF16),
            jax.ShapeDtypeStruct((NX, *shard), BF16),
            jax.ShapeDtypeStruct((PAIRS,), jnp.int32),
        ),
        in_specs=[hbm] * 10,
        out_specs=(hbm,) * 5,
        scratch_shapes=[
            smem(PAIRS), smem(PAIRS), smem(2), smem(2), smem(PAIRS), smem(PAIRS), smem(PAIRS), smem(2 * PAIRS), smem(NEXT),
            bf(*w1.shape), bf(*w2.shape), bf(*w3.shape), bf(*node.shape), bf(*cot.shape), bf(*edge.shape), bf(PAIRS * BLOCK, D),
            lent, bf(NY, NZH, 2, *shard), lent,
            bf(3 * D, D), bf(3 * D, D), bf(D, D), bf(D, D), bf(D, D),
            f32(NEXT, BLOCK, D), f32(NEXT, BLOCK, D), bf(NEXT, BLOCK, D),
            f32(2 * PAIRS + 1, BLOCK, D), f32(2, 2 * PAIRS + 1, BLOCK, D),
            bf(steps, 2 * rows, D), f32(2 * rows, D), bf(steps, rows, D), bf(steps, 2 * rows, D),
            bf(steps, rows, D), bf(steps, rows, D),
            f32(3 * D, D), f32(D, D), f32(D, D), bf(NY, NZH, 2, *shard), lent, blocks, blocks,
            lent, bf(NY, NZH, *shard), bf(NY, NZH, *shard), bf(NY - 1, NZH, *shard), bf(NZH, *shard),
            bf(NZ, *shard), bf(*shard),
            bf(*node.shape), bf(*cot.shape), bf(PAIRS * BLOCK, D),
            dma((5,)), dma((10,)), dma((NZ - 1,)), dma((NZH,)), dma((NZH, NY - 1)), dma((NY, NZH)),
            dma((NY * NZH,)), dma((NY, NZH)), dma((NH,)), dma((NH,)), dma((NH,)), dma((NH,)),
            dma((2,)), dma((2,)), dma((2, NY - 1)), dma((2, NY - 1)),
            dma((NZH,)), dma((NZ,)), dma((2 * NX - 1,)), dma((NX,)),
        ],
        compiler_params=pltpu.CompilerParams(
            collective_id=0, has_side_effects=True, vmem_limit_bytes=VMEM_MIB << 20
        ),
        name="layer",
    )(near, far, sf, sd, w1, w2, w3, node, cot, edge)


def results_kernel(
    order_hbm, state, grad, edges, total, out_state, out_grad, out_edges, out_1, out_2, out_3,
    order, state_v, grad_v, edges_v, sum_v, total_v, order_sem, in_sem, out_sem,
):
    order_copy = pltpu.make_async_copy(order_hbm, order, order_sem)
    order_copy.start()
    quarter = CHUNK * BLOCK
    spans = [pl.ds(i * quarter, quarter) for i in range(PAIRS // CHUNK)]
    loads = [
        pltpu.make_async_copy(src, held, in_sem.at[i])
        for i, (src, held) in enumerate(
            [(edges.at[s], edges_v.at[s]) for s in spans]
            + [(state, state_v), (grad, grad_v), (total, sum_v)]
        )
    ]
    for load in loads:
        load.start()
    order_copy.wait()
    stores = []

    def store(src, dst):
        copy = pltpu.make_async_copy(src, dst, out_sem.at[len(stores)])
        copy.start()
        stores.append(copy)

    for i in range(PAIRS):
        if i % CHUNK == 0:
            loads[i // CHUNK].wait()
        rows = pl.ds(pl.multiple_of(order[i] * BLOCK, BLOCK), BLOCK)
        store(edges_v.at[pl.ds(i * BLOCK, BLOCK)], out_edges.at[rows])
    loads[4].wait()
    store(state_v, out_state)
    loads[5].wait()
    store(grad_v, out_grad)
    loads[6].wait()
    total_v[...] = sum((sum_v[i].astype(F32) for i in range(1, NX)), sum_v[0].astype(F32))
    store(total_v.at[0:3], out_1)
    store(total_v.at[3], out_2)
    store(total_v.at[4], out_3)
    for copy in stores:
        copy.wait()


def results(order, state, grad, edges, total):
    hbm = pl.BlockSpec(memory_space=pltpu.HBM)
    dma = pltpu.SemaphoreType.DMA
    return pl.pallas_call(
        results_kernel,
        out_shape=(
            jax.ShapeDtypeStruct(state.shape, BF16),
            jax.ShapeDtypeStruct(grad.shape, BF16),
            jax.ShapeDtypeStruct(edges.shape, BF16),
            jax.ShapeDtypeStruct((3, 8, D), F32),
            jax.ShapeDtypeStruct((8, D), F32),
            jax.ShapeDtypeStruct((8, D), F32),
        ),
        in_specs=[hbm] * 5,
        out_specs=(hbm,) * 6,
        scratch_shapes=[
            pltpu.SMEM((PAIRS,), jnp.int32),
            pltpu.VMEM(state.shape, BF16), pltpu.VMEM(grad.shape, BF16),
            pltpu.VMEM(edges.shape, BF16), pltpu.VMEM(total.shape, BF16), pltpu.VMEM(total.shape[1:], F32),
            dma, dma((7,)), dma((PAIRS + 5,)),
        ],
        compiler_params=pltpu.CompilerParams(vmem_limit_bytes=VMEM_MIB << 20),
        name="results",
    )(order, state, grad, edges, total)


def body(node_state, edge_state, cotangent, w_first, w_second, w_third,
         pair_near, pair_far, send_fsdp, send_dom):
    new_state, grad_state, grad_edges, total, order = layer(
        pair_near, pair_far, send_fsdp.reshape(2), send_dom.reshape(2), w_first, w_second, w_third,
        node_state.reshape(NBD, BLOCK, D), cotangent.reshape(NBD, BLOCK, D),
        edge_state.reshape(PAIRS, BLOCK, D),
    )
    new_state, grad_state, grad_edges, g1, g2, g3 = results(
        order, new_state, grad_state, grad_edges, total
    )
    return (
        new_state.reshape(NBD * BLOCK, D),
        grad_state.reshape(NBD * BLOCK, D),
        grad_edges,
        g1.reshape(24, D),
        g2,
        g3,
    )


def solution(mesh):
    cells = P(("dom", "fsdp"), None)
    rows = P("fsdp", None)
    flat = P(("dom", "fsdp"))
    lists = P(("dom", "fsdp"), None, None)
    return jax.shard_map(
        body,
        mesh=mesh,
        in_specs=(cells, cells, cells, rows, rows, rows, flat, flat, lists, lists),
        out_specs=(cells, cells, cells, rows, rows, rows),
        check_vma=False,
    )
```

```python
import jax
import jax.numpy as jnp
from jax import lax
from jax.experimental import pallas as pl
from jax.experimental.pallas import tpu as pltpu
from jax.sharding import PartitionSpec as P

BLOCK = 128
D = 256
NBD = 6
NH = 4
NEXT = NBD + NH
PAIRS = 16
NX, NY, NZ = 4, 4, 8
NZH = NZ // 2
UNITS = 5
CHUNK = 4
UNROLL = True
VMEM_MIB = 58
LENT_CHUNK = 2
MESH = pl.DeviceIdType.MESH
F32, BF16 = jnp.float32, jnp.bfloat16


def place():
    a = lax.axis_index("dom")
    f = lax.axis_index("fsdp")
    return a, f, a // 2, lax.rem(a, 2), f // NZ, lax.rem(f, NZ)


def halo_peers(a, f):
    nd, nf = 2 * NX, NY * NZ
    return (
        (a, lax.rem(f + nf - 1, nf)),
        (a, lax.rem(f + 1, nf)),
        (lax.rem(a + nd - 1, nd), f),
        (lax.rem(a + 1, nd), f),
    )


def signal_all(peers):
    barrier = pltpu.get_barrier_semaphore()
    for peer in peers:
        pl.semaphore_signal(barrier, inc=1, device_id=peer, device_id_type=MESH)


def wait_all(count):
    pl.semaphore_wait(pltpu.get_barrier_semaphore(), count)


def remote(src, dst, send, recv, peer):
    return pltpu.make_async_remote_copy(
        src_ref=src, dst_ref=dst, send_sem=send, recv_sem=recv,
        device_id=peer, device_id_type=MESH,
    )


def mm(p, q):
    return jnp.dot(p, q, preferred_element_type=F32)


def mm_t(p, q):
    return lax.dot_general(p, q, (((1,), (1,)), ((), ())), preferred_element_type=F32)


def t_mm(p, q):
    return lax.dot_general(p, q, (((0,), (0,)), ((), ())), preferred_element_type=F32)


def act_slope(half):
    up = 1.0 + jnp.tanh(half)
    act = half * up
    return act, up + act * (2.0 - up)


def layer_kernel(
    near_hbm, far_hbm, sf_hbm, sd_hbm, w1_hbm, w2_hbm, w3_hbm, node_hbm, cot_hbm, edge_hbm,
    state_out, grad_out, edge_out, pieces_out, order_out,
    near_in, far_in, sf, sd, order, near, far, chain, last, w1s, w2s, w3s, node, cot, edge_in, edge, lend, wall, halo,
    w1, w1h, w2h, w3, w3h, left, right, ctab, tsum, ysum, a1, d1, gg, sg, dd, ef,
    first, acc_2, acc_3, grads, back, state_part, grad_part,
    got, sibbuf, q, ybuf, r, zbuf, fin, new_state, grad_state, ge,
    os, ls, zs, zr, ys, yr, ss, sr, hs, hr, bs, br, s0, r0, y2s, y2r, z2s, z2r, fs, fr,
):
    a, f, x, c, y, z = place()
    zh, zc = z // 2, lax.rem(z, 2)
    sib = (a + 1 - 2 * c, f)
    ypeers = [(a, lax.rem(y + d, NY) * NZ + z) for d in range(1, NY)]
    zpeers = [(a, y * NZ + lax.rem(z + d, NZ)) for d in range(1, NZ)]
    dpeers = [(lax.rem(a + d, 2 * NX), f) for d in range(1, 2 * NX)]
    hpeers = halo_peers(a, f)
    everyone = [zpeers[d] for d in (3, 2, 4, 1, 5, 0, 6)] + ypeers + dpeers + list(hpeers[:2])
    signal_all(everyone)

    loads = [
        pltpu.make_async_copy(src, dst, ls.at[i])
        for i, (src, dst) in enumerate((
            (w1_hbm, w1s), (w2_hbm, w2s), (w3_hbm, w3s), (sf_hbm, sf), (sd_hbm, sd),
            (node_hbm, node), (cot_hbm, cot), (near_hbm, near_in), (far_hbm, far_in), (edge_hbm, edge_in),
        ))
    ]
    for copy in loads:
        copy.start()
    for copy in loads[:3]:
        copy.wait()

    @pl.when(zc == c)
    def _():
        wall[y, zh, c, 0:3] = w1s[...].astype(F32).reshape(3, 8, D).astype(BF16)
        wall[y, zh, c, 3] = w2s[...]
        wall[y, zh, c, 4] = w3s[...]

    for copy in loads[3:7]:
        copy.wait()
    for s in range(2):
        b = sf[s]
        lend[s, 0] = node[b]
        lend[s, 1] = cot[b]
        b = sd[s]
        lend[2 + s, 0] = node[b]
        lend[2 + s, 1] = cot[b]
    wait_all(len(everyone))

    halos = [
        remote(lend.at[s], halo.at[s ^ 1], hs.at[s], hr.at[s ^ 1], hpeers[s])
        for s in range(NH)
    ]
    zcopies = [
        remote(wall.at[y, zh, c], wall.at[y, zh, c], zs.at[d], zr.at[zh], zpeers[d])
        for d in (3, 2, 4, 1, 5, 0, 6)
    ]

    @pl.when(zc == c)
    def _():
        for copy in zcopies:
            copy.start()

    halos[2].start()
    halos[3].start()

    loads[7].wait()
    loads[8].wait()
    count, place_of = jnp.int32(0), []
    for p in range(PAIRS):
        entry = far_in[p]
        own_place = count + jnp.where(count < LENT_CHUNK * CHUNK, 0, CHUNK)
        place_of.append(jnp.where(entry < NBD, own_place, entry + (LENT_CHUNK * CHUNK - NBD)))
        count = count + jnp.where(entry < NBD, 1, 0)

    def arrange(i, carry):
        pair, near_i, far_i = jnp.int32(0), near_in[0], far_in[0]
        for p in range(1, PAIRS):
            here = place_of[p] == i
            pair = jnp.where(here, p, pair)
            near_i = jnp.where(here, near_in[p], near_i)
            far_i = jnp.where(here, far_in[p], far_i)
        order[i] = pair
        near[i] = near_i
        far[i] = far_i
        return carry

    lax.fori_loop(0, PAIRS, arrange, 0)

    keys = [(near, far)[h % 2][h // 2] for h in range(2 * PAIRS)]

    def link(h, carry):
        p = h // 2
        key = jnp.where(lax.rem(h, 2) == 0, near[p], far[p])
        before = jnp.int32(2 * PAIRS)
        for g in range(2 * PAIRS):
            before = jnp.where((keys[g] == key) & (g < h), g, before)
        chain[h] = before
        return carry

    lax.fori_loop(0, 2 * PAIRS, link, 0)

    def end(b, carry):
        where = jnp.int32(2 * PAIRS)
        for g in range(2 * PAIRS):
            where = jnp.where(keys[g] == b, g, where)
        last[b] = where
        return carry

    lax.fori_loop(0, NEXT, end, 0)

    sent = []

    def pass_on(yy, h, slot, along_y):
        part = wall.at[yy, h, c]
        if along_y:
            for d, peer in enumerate(ypeers):
                copy = remote(part, part, ys.at[slot, d], yr.at[y, h], peer)
                copy.start()
                sent.append(copy)
        copy = remote(part, part, ss.at[slot], sr.at[yy, h], sib)
        copy.start()
        sent.append(copy)

    for i, d in enumerate((0, 1, 3, 2)):
        h = lax.rem(zh + d, NZH)

        @pl.when(2 * h + c != z)
        def _():
            part = wall.at[y, h, c]
            remote(part, part, zs.at[0], zr.at[h], sib).wait_recv()

        pass_on(y, h, i, True)

    tsum[2 * PAIRS] = jnp.zeros((BLOCK, D), F32)
    ysum[0, 2 * PAIRS] = jnp.zeros((BLOCK, D), F32)
    ysum[1, 2 * PAIRS] = jnp.zeros((BLOCK, D), F32)
    ctab[0:NBD] = cot[...]

    for i, d in enumerate((0, 1, 3, 2)):
        h = lax.rem(zh + d, NZH)
        for e in (1, 3, 2):
            yy = lax.rem(y + e, NY)
            part = wall.at[yy, h, c]
            remote(part, part, ys.at[0, 0], yr.at[yy, h], sib).wait_recv()
            pass_on(yy, h, 4 * e + i, False)
    halos[0].start()
    halos[1].start()
    loads[9].wait()
    rows = CHUNK * BLOCK
    direct = [slice(j * BLOCK, (j + 1) * BLOCK) for j in range(CHUNK)]
    mirror = [slice(rows + j * BLOCK, rows + (j + 1) * BLOCK) for j in range(CHUNK)]
    own_rows = NBD * BLOCK
    for yy in range(NY):
        for h in range(NZH):
            part = wall.at[yy, h, 1 - c]
            remote(part, part, ss.at[0], sr.at[yy, h], sib).wait_recv()

    packed = wall[...].reshape(NY * NZ, UNITS, 8, D).astype(F32)
    flat = packed[:, 0:3].reshape(3 * D, D)
    w1[...] = flat.astype(BF16)
    w1h[...] = (0.5 * flat).astype(BF16)
    w2h[...] = (0.5 * packed[:, 3].reshape(D, D)).astype(BF16)
    third = packed[:, 4].reshape(D, D)
    w3[...] = third.astype(BF16)
    w3h[...] = (0.5 * third).astype(BF16)
    own = node[...].reshape(own_rows, D)
    for table, cols in ((left, 0), (right, D)):
        table[0:NBD] = mm(own, w1h[cols:cols + D]).reshape(NBD, BLOCK, D)

    def part_of(ref, steps):
        return ref[0:steps].reshape(-1, D)

    def chunk(i, carry):
        pairs = [i * CHUNK + j for j in range(CHUNK)]
        ends = [(near[p], far[p]) for p in pairs]
        links = [(2 * p, chain[2 * p], chain[2 * p + 1]) for p in pairs]
        span = pl.ds(pl.multiple_of(i * rows, rows), rows)
        for j, p in enumerate(pairs):
            edge[pl.ds(pl.multiple_of(p * BLOCK, BLOCK), BLOCK)] = edge_in[order[p]]
        edge_part = mm(edge[span], w1h[2 * D:])
        for j, (n, m) in enumerate(ends):
            gg[i, direct[j]] = (ctab[n].astype(F32) - ctab[m].astype(F32)).astype(BF16)
            for where, p, k in ((direct[j], n, m), (mirror[j], m, n)):
                act, slope = act_slope(left[p] + right[k] + edge_part[direct[j]])
                a1[i, where] = act.astype(BF16)
                d1[where] = slope.astype(BF16)
        second = mm(a1[i], w2h[...])
        back_3 = mm_t(gg[i], w3h[...])
        for j, (h, before_n, before_m) in enumerate(links):
            act_f, slope_f = act_slope(second[direct[j]])
            act_m, slope_m = act_slope(second[mirror[j]])
            diff = act_f - act_m
            dd[i, direct[j]] = diff.astype(BF16)
            tsum[h] = tsum[before_n] + diff
            tsum[h + 1] = tsum[before_m] - diff
            sg[i, direct[j]] = (back_3[direct[j]] * slope_f).astype(BF16)
            sg[i, mirror[j]] = (-back_3[direct[j]] * slope_m).astype(BF16)
        first_back = mm_t(sg[i], w2h[...])
        for j, (h, before_n, before_m) in enumerate(links):
            part_f = first_back[direct[j]] * d1[direct[j]].astype(F32)
            part_m = first_back[mirror[j]] * d1[mirror[j]].astype(F32)
            ef[i, direct[j]] = (part_f + part_m).astype(BF16)
            ysum[0, h] = ysum[0, before_n] + part_f
            ysum[0, h + 1] = ysum[0, before_m] + part_m
            ysum[1, h] = ysum[1, before_n] + part_m
            ysum[1, h + 1] = ysum[1, before_m] + part_f
        ge[span] = mm_t(ef[i], w1[2 * D:]).astype(BF16)
        return carry

    final = PAIRS // CHUNK - 1
    lax.fori_loop(0, LENT_CHUNK, chunk, 0, unroll=UNROLL)

    for s in range(NH):
        halos[s].wait_recv()
    ctab[NBD:] = halo[:, 1]
    lent = halo[:, 0].reshape(NH * BLOCK, D)
    for table, cols in ((left, 0), (right, D)):
        table[NBD:] = mm(lent, w1h[cols:cols + D]).reshape(NH, BLOCK, D)
    chunk(LENT_CHUNK, 0)

    wa, wb = w1[0:D], w1[D:2 * D]
    lent_ends = [2 * (LENT_CHUNK * CHUNK + k) + 1 for k in range(NH)]

    def lent_sum(ref):
        return jnp.concatenate([ref[h].astype(BF16) for h in lent_ends], 0)

    lent_flux = mm(lent_sum(tsum), w3[...])
    lent_grad = mm_t(lent_sum(ysum.at[0]), wa) + mm_t(lent_sum(ysum.at[1]), wb)
    back[:, 0] = lent_flux.astype(BF16).reshape(NH, BLOCK, D)
    back[:, 1] = lent_grad.astype(BF16).reshape(NH, BLOCK, D)
    backs = [
        remote(back.at[s], got.at[s ^ 1], bs.at[s], br.at[s ^ 1], hpeers[s])
        for s in range(NH)
    ]
    for copy in backs:
        copy.start()

    lax.fori_loop(LENT_CHUNK + 1, PAIRS // CHUNK, chunk, 0, unroll=UNROLL)
    first[2 * D:] = t_mm(edge[0:final * rows], part_of(ef, final))
    acc_2[...] = t_mm(part_of(a1, final), part_of(sg, final))
    acc_3[...] = t_mm(part_of(dd, final), part_of(gg, final))
    stores = [
        pltpu.make_async_copy(src, dst, os.at[i])
        for i, (src, dst) in enumerate((
            (ge, edge_out), (new_state, state_out), (grad_state, grad_out),
        ))
    ]
    stores[0].start()
    order_store = pltpu.make_async_copy(order, order_out, os.at[4])
    order_store.start()

    ends = [last[b] for b in range(NEXT)]

    def gathered(pick):
        return jnp.concatenate([pick(h).astype(BF16) for h in ends], 0)

    ts = gathered(lambda h: tsum[h])
    ya = gathered(lambda h: ysum[0, h])
    yb = gathered(lambda h: ysum[1, h])

    pieces = (slice(3, 5), slice(0, 3))

    def to_sibling(k):
        copy = remote(grads.at[:, :, 1 - c, pieces[k]], sibbuf.at[:, :, pieces[k]], s0.at[k], r0.at[k], sib)
        copy.start()
        return copy

    grads[:, :, :, 3] = (acc_2[...] + t_mm(a1[final], sg[final])).reshape(NY, NZH, 2, 8, D).astype(BF16)
    grads[:, :, :, 4] = (acc_3[...] + t_mm(dd[final], gg[final])).reshape(NY, NZH, 2, 8, D).astype(BF16)
    cores = [to_sibling(0)]
    first[0:D] = t_mm(own, ya[:own_rows]) + t_mm(lent, ya[own_rows:])
    first[D:2 * D] = t_mm(own, yb[:own_rows]) + t_mm(lent, yb[own_rows:])
    first[2 * D:] += t_mm(edge[final * rows:], ef[final])
    grads[:, :, :, 0:3] = first[...].reshape(NY, NZH, 2, 3, 8, D).astype(BF16)
    cores.append(to_sibling(1))

    ycopies = []
    for k, piece in enumerate(pieces):
        cores[k].wait_recv()
        q[:, :, piece] = (grads[:, :, c, piece].astype(F32) + sibbuf[:, :, piece].astype(F32)).astype(BF16)
        for d, peer in enumerate(ypeers):
            yy = lax.rem(y + d + 1, NY)
            copy = remote(q.at[yy, :, piece], ybuf.at[d, :, piece], y2s.at[k, d], y2r.at[k, d], peer)
            copy.start()
            ycopies.append(copy)

    flux = mm(ts[:own_rows], w3[...]).reshape(NBD, BLOCK, D)
    state_part[...] = node[...].astype(F32) + flux
    node_grad = mm_t(ya[:own_rows], wa) + mm_t(yb[:own_rows], wb)
    grad_part[...] = cot[...].astype(F32) + node_grad.reshape(NBD, BLOCK, D)

    @pl.when(zc == c)
    def _():
        for copy in zcopies:
            copy.wait_send()

    for copy in sent + halos:
        copy.wait_send()
    stores[0].wait()
    order_store.wait()

    value = q[y].astype(F32)
    for copy in ycopies:
        copy.wait_recv()
    for d in range(NY - 1):
        value = value + ybuf[d].astype(F32)
    r[...] = value.astype(BF16)

    rcopies = []
    for k, d in enumerate((2, 1, 3, 0)):
        h = lax.rem(zh + d, NZH)
        copy = remote(r.at[h], zbuf.at[z], z2s.at[k], z2r.at[z], (a, y * NZ + 2 * h + c))
        rcopies.append((h, copy))

        @pl.when(2 * h + c != z)
        def _():
            copy.start()

    for copy in backs:
        copy.wait_recv()
    owner = (sf[0], sf[1], sd[0], sd[1])

    def settle(k, part, out):
        for b in range(NBD):
            value = part[b]
            for s in range(NH):
                value = value + jnp.where(owner[s] == b, got[s, k].astype(F32), 0.0)
            out[b] = value.astype(BF16)

    settle(0, state_part, new_state)
    stores[1].start()
    settle(1, grad_part, grad_state)
    stores[2].start()

    for copy in backs + cores + ycopies:
        copy.wait_send()
    for h, copy in rcopies:
        @pl.when(2 * h + c != z)
        def _():
            copy.wait_send()
    for copy in stores[1:]:
        copy.wait()

    fcopies = [
        remote(fin, pieces_out.at[x], fs.at[d], fr.at[x], dpeers[d]) for d in (3, 4, 2, 5, 1, 6, 0)
    ]

    @pl.when(zc == c)
    def _():
        acc = r[zh].astype(F32)
        for d in (1, 7, 2, 6, 3, 5, 4):
            zz = lax.rem(z + d, NZ)
            remote(r.at[0], zbuf.at[zz], z2s.at[0], z2r.at[zz], sib).wait_recv()
            acc = acc + zbuf[zz].astype(F32)
        fin[...] = acc.astype(BF16)
        for copy in fcopies:
            copy.start()
        own_piece = pltpu.make_async_copy(fin, pieces_out.at[x], os.at[3])
        own_piece.start()
        for copy in fcopies:
            copy.wait_send()
        own_piece.wait()

    @pl.when(zc != c)
    def _():
        remote(fin, pieces_out.at[x], fs.at[0], fr.at[x], sib).wait_recv()

    for d in range(1, NX):
        xx = lax.rem(x + d, NX)
        remote(fin, pieces_out.at[xx], fs.at[0], fr.at[xx], sib).wait_recv()


def layer(near, far, sf, sd, w1, w2, w3, node, cot, edge):
    hbm = pl.BlockSpec(memory_space=pltpu.HBM)
    dma = pltpu.SemaphoreType.DMA
    steps, rows = PAIRS // CHUNK, CHUNK * BLOCK
    shard = (UNITS, 8, D)

    def smem(count):
        return pltpu.SMEM((count,), jnp.int32)

    def bf(*shape):
        return pltpu.VMEM(shape, BF16)

    def f32(*shape):
        return pltpu.VMEM(shape, F32)

    lent = bf(NH, 2, BLOCK, D)
    blocks = f32(NBD, BLOCK, D)
    return pl.pallas_call(
        layer_kernel,
        out_shape=(
            jax.ShapeDtypeStruct(node.shape, BF16),
            jax.ShapeDtypeStruct(cot.shape, BF16),
            jax.ShapeDtypeStruct((PAIRS * BLOCK, D), BF16),
            jax.ShapeDtypeStruct((NX, *shard), BF16),
            jax.ShapeDtypeStruct((PAIRS,), jnp.int32),
        ),
        in_specs=[hbm] * 10,
        out_specs=(hbm,) * 5,
        scratch_shapes=[
            smem(PAIRS), smem(PAIRS), smem(2), smem(2), smem(PAIRS), smem(PAIRS), smem(PAIRS), smem(2 * PAIRS), smem(NEXT),
            bf(*w1.shape), bf(*w2.shape), bf(*w3.shape), bf(*node.shape), bf(*cot.shape), bf(*edge.shape), bf(PAIRS * BLOCK, D),
            lent, bf(NY, NZH, 2, *shard), lent,
            bf(3 * D, D), bf(3 * D, D), bf(D, D), bf(D, D), bf(D, D),
            f32(NEXT, BLOCK, D), f32(NEXT, BLOCK, D), bf(NEXT, BLOCK, D),
            f32(2 * PAIRS + 1, BLOCK, D), f32(2, 2 * PAIRS + 1, BLOCK, D),
            bf(steps, 2 * rows, D), bf(2 * rows, D), bf(steps, rows, D), bf(steps, 2 * rows, D),
            bf(steps, rows, D), bf(steps, rows, D),
            f32(3 * D, D), f32(D, D), f32(D, D), bf(NY, NZH, 2, *shard), lent, blocks, blocks,
            lent, bf(NY, NZH, *shard), bf(NY, NZH, *shard), bf(NY - 1, NZH, *shard), bf(NZH, *shard),
            bf(NZ, *shard), bf(*shard),
            bf(*node.shape), bf(*cot.shape), bf(PAIRS * BLOCK, D),
            dma((5,)), dma((10,)), dma((NZ - 1,)), dma((NZH,)), dma((NZH, NY - 1)), dma((NY, NZH)),
            dma((NY * NZH,)), dma((NY, NZH)), dma((NH,)), dma((NH,)), dma((NH,)), dma((NH,)),
            dma((2,)), dma((2,)), dma((2, NY - 1)), dma((2, NY - 1)),
            dma((NZH,)), dma((NZ,)), dma((2 * NX - 1,)), dma((NX,)),
        ],
        compiler_params=pltpu.CompilerParams(
            collective_id=0, has_side_effects=True, vmem_limit_bytes=VMEM_MIB << 20
        ),
        name="layer",
    )(near, far, sf, sd, w1, w2, w3, node, cot, edge)


def results_kernel(
    order_hbm, state, grad, edges, total, out_state, out_grad, out_edges, out_1, out_2, out_3,
    order, state_v, grad_v, edges_v, sum_v, total_v, order_sem, in_sem, out_sem,
):
    order_copy = pltpu.make_async_copy(order_hbm, order, order_sem)
    order_copy.start()
    quarter = CHUNK * BLOCK
    spans = [pl.ds(i * quarter, quarter) for i in range(PAIRS // CHUNK)]
    loads = [
        pltpu.make_async_copy(src, held, in_sem.at[i])
        for i, (src, held) in enumerate(
            [(edges.at[s], edges_v.at[s]) for s in spans]
            + [(state, state_v), (grad, grad_v), (total, sum_v)]
        )
    ]
    for load in loads:
        load.start()
    order_copy.wait()
    stores = []

    def store(src, dst):
        copy = pltpu.make_async_copy(src, dst, out_sem.at[len(stores)])
        copy.start()
        stores.append(copy)

    for i in range(PAIRS):
        if i % CHUNK == 0:
            loads[i // CHUNK].wait()
        rows = pl.ds(pl.multiple_of(order[i] * BLOCK, BLOCK), BLOCK)
        store(edges_v.at[pl.ds(i * BLOCK, BLOCK)], out_edges.at[rows])
    loads[4].wait()
    store(state_v, out_state)
    loads[5].wait()
    store(grad_v, out_grad)
    loads[6].wait()
    total_v[...] = sum((sum_v[i].astype(F32) for i in range(1, NX)), sum_v[0].astype(F32))
    store(total_v.at[0:3], out_1)
    store(total_v.at[3], out_2)
    store(total_v.at[4], out_3)
    for copy in stores:
        copy.wait()


def results(order, state, grad, edges, total):
    hbm = pl.BlockSpec(memory_space=pltpu.HBM)
    dma = pltpu.SemaphoreType.DMA
    return pl.pallas_call(
        results_kernel,
        out_shape=(
            jax.ShapeDtypeStruct(state.shape, BF16),
            jax.ShapeDtypeStruct(grad.shape, BF16),
            jax.ShapeDtypeStruct(edges.shape, BF16),
            jax.ShapeDtypeStruct((3, 8, D), F32),
            jax.ShapeDtypeStruct((8, D), F32),
            jax.ShapeDtypeStruct((8, D), F32),
        ),
        in_specs=[hbm] * 5,
        out_specs=(hbm,) * 6,
        scratch_shapes=[
            pltpu.SMEM((PAIRS,), jnp.int32),
            pltpu.VMEM(state.shape, BF16), pltpu.VMEM(grad.shape, BF16),
            pltpu.VMEM(edges.shape, BF16), pltpu.VMEM(total.shape, BF16), pltpu.VMEM(total.shape[1:], F32),
            dma, dma((7,)), dma((PAIRS + 5,)),
        ],
        compiler_params=pltpu.CompilerParams(vmem_limit_bytes=VMEM_MIB << 20),
        name="results",
    )(order, state, grad, edges, total)


def body(node_state, edge_state, cotangent, w_first, w_second, w_third,
         pair_near, pair_far, send_fsdp, send_dom):
    new_state, grad_state, grad_edges, total, order = layer(
        pair_near, pair_far, send_fsdp.reshape(2), send_dom.reshape(2), w_first, w_second, w_third,
        node_state.reshape(NBD, BLOCK, D), cotangent.reshape(NBD, BLOCK, D),
        edge_state.reshape(PAIRS, BLOCK, D),
    )
    new_state, grad_state, grad_edges, g1, g2, g3 = results(
        order, new_state, grad_state, grad_edges, total
    )
    return (
        new_state.reshape(NBD * BLOCK, D),
        grad_state.reshape(NBD * BLOCK, D),
        grad_edges,
        g1.reshape(24, D),
        g2,
        g3,
    )


def solution(mesh):
    cells = P(("dom", "fsdp"), None)
    rows = P("fsdp", None)
    flat = P(("dom", "fsdp"))
    lists = P(("dom", "fsdp"), None, None)
    return jax.shard_map(
        body,
        mesh=mesh,
        in_specs=(cells, cells, cells, rows, rows, rows, flat, flat, lists, lists),
        out_specs=(cells, cells, cells, rows, rows, rows),
        check_vma=False,
    )
```
